512 devices in a mesh: prefix: 64 (over z, x), tensor: 8 (over y, core).
Axes of the slice: x: 4, y: 4, z: 16, core: 2. Of those that a mesh axis runs over, the one named last changes fastest.
Arguments:
- queries: bfloat16 [4096, 3, 4096], P('prefix', None, 'tensor'), may hold values from -100 to 100
- prefix_cache: bfloat16 [64, 8, 128, 2304], P('prefix', 'tensor'), may hold values from -10 to 10
- suffix_cache: bfloat16 [4096, 8, 128, 80], P('prefix', 'tensor'), may hold values from -10 to 10
- suffix_lengths: int32 [4096], P('prefix'), may hold values from 50 to 80, as said below
- request_prefix: int32 [4096, 1], replicated, may hold values from 0 to 63; in each aligned block of 64 rows (0 to 63, 64 to 127, ...) at most 2 rows name the same one
- prefix_owner: int32 [64], replicated, may hold values from 0 to 63, each once
- out_proj: bfloat16 [4096, 2880], P('tensor'), may hold values from -0.25 to 0.25
Outputs:
- output: bfloat16 [4096, 3, 2880], P('prefix', None, 'tensor')
The draws below stay inside these ranges and needn't reach their ends.
Inputs may be any that keep to these rules, and one draw needn't show every extreme that they name: `request_prefix`: the requests of one device name any one prefix at most 2 times. `prefix_owner`: each stored index holds exactly one prefix. `suffix_lengths`: every device homes a request whose suffix cache is full.
All inputs are finite; a program needn't handle non-finite values.
Results may differ from the reference program's by a relative error of at most 0.017.
Values may be sent and summed in bfloat16 or wider, within the bound.
No kernel may reach another device: no remote copies, remote signals or barrier semaphores. Data moves between devices by JAX's collectives and lax.ppermute only.
A program may use at most 128 MiB of HBM per device.

```python
import math
import jax
import jax.numpy as jnp
import numpy as np
from jax import lax

HEADS = 64
KVH = 8
HD = 64
WIDTH = 2880
REQ_DEV = 64
PLEN = 2304
SUF = 80
STEPS = 3
REQUESTS = 4096
PREFIXES = 64
CAP = 2
N_TENSOR = 8


def draw_queries(key, part):
    key = jax.random.fold_in(key, 3)
    key_normal = jax.random.fold_in(key, 0)
    extent = (REQUESTS, STEPS, HEADS, HD)
    normal_part = 2.0 * jnp.clip(jax.random.normal(key_normal, extent, jnp.float32), -6.0, 6.0)
    return normal_part.reshape(REQUESTS, STEPS, HEADS * HD).astype(jnp.bfloat16)


def cache_entries(key, lead, length):
    key_noise = jax.random.fold_in(key, 0)
    extent = (lead, KVH, 2 * HD, length)
    entries = jnp.clip(jax.random.normal(key_noise, extent, jnp.float32), -6.0, 6.0)
    return entries.astype(jnp.bfloat16)


def draw_prefix_cache(key, part):
    return cache_entries(jax.random.fold_in(key, 1), PREFIXES, PLEN)


def draw_suffix_cache(key, part):
    return cache_entries(jax.random.fold_in(key, 2), REQUESTS, SUF)


def draw_suffix_lengths(key, part):
    key = jax.random.fold_in(key, 4)
    lengths = jax.random.randint(key, (REQUESTS,), SUF * 5 // 8, SUF + 1, jnp.int32)
    first_rows = jnp.arange(REQUESTS, dtype=jnp.int32) % REQ_DEV == 0
    return jnp.where(first_rows, SUF, lengths).astype(jnp.int32)


def block_scale(stream_key, shape, shards, least, high):
    def one(dim, shards_of):
        draws = jax.random.uniform(jax.random.fold_in(jax.random.fold_in(stream_key, 6), dim), (shards_of,), jnp.float32, least / len(shards), high / len(shards))
        return jnp.repeat(jnp.exp(draws), shape[dim] // shards_of).reshape((-1,) + (1,) * (len(shape) - dim - 1))

    loudness = one(*shards[0])
    for cut in shards[1:]:
        loudness = loudness * one(*cut)
    return loudness


def deal_out(key, own, number, rows, amount, top, bound, skew):
    ranking = jax.random.permutation(key, amount)
    packed, usual = shares(amount, rows * top, bound, skew, True), shares(amount, rows * top, bound, skew, False)
    places = jnp.arange(amount)

    def named(tallies, rotation):
        used = int((tallies > 0).sum())
        fixed = max(1, used // 4)
        moved = fixed + (places - fixed + rotation * (used - fixed)) % max(1, amount - fixed)
        return jnp.zeros((amount,), jnp.int32).at[ranking[jnp.where(places < fixed, places, moved)]].set(jnp.asarray(tallies, jnp.int32))

    tallies = jnp.where(number % 4 == 0, named(packed, number // 4), named(usual, number - number // 4 - 1))
    mixed = jax.random.permutation(jax.random.fold_in(own, 3), amount)
    donor, taker = mixed[0:amount // 2 * 2:2], mixed[1:amount // 2 * 2:2]
    room = jnp.minimum(tallies[donor] - 1, bound - tallies[taker]) // 2
    room = jnp.where((donor == ranking[0]) | (taker == ranking[0]) | (tallies[taker] == 0), 0, jnp.maximum(room, 0))
    moved = jax.random.randint(jax.random.fold_in(own, 4), (amount // 2,), 0, 1 << 20) % (room + 1)
    tallies = tallies.at[donor].add(-moved).at[taker].add(moved)
    items = jnp.searchsorted(jnp.cumsum(tallies), jnp.arange(rows * top), side="right").astype(jnp.int32)
    table = items.reshape(top, rows).T
    table = table[jax.random.permutation(jax.random.fold_in(own, 1), rows)]
    rotation = jax.random.randint(jax.random.fold_in(own, 2), (rows, 1), 0, top)
    return jnp.take_along_axis(table, (jnp.arange(top)[None, :] + rotation) % top, axis=1)


def shares(number_of, total, bound, skew, full):
    loads = [(1 << 20) // math.isqrt(standing ** skew) + 1 for standing in range(1, number_of + 1)]
    largest = bound if full else min(bound, max(-(-total // number_of), total * loads[0] // sum(loads)))
    least = 1 if total - largest >= number_of - 1 else 0
    holding, rest = [largest] + [least] * (number_of - 1), total - largest - least * (number_of - 1)
    while rest > 0:
        candidates = [i for i in range(1, number_of) if holding[i] < largest] or [i for i in range(1, number_of) if holding[i] < bound]
        pool, remaining = sum([loads[i] for i in candidates]), rest
        for i in candidates:
            extra = min(bound - holding[i], max(1, remaining * loads[i] // pool), rest)
            holding[i] = holding[i] + extra
            rest = rest - extra
    return np.array(holding)


def scatter_about(own_key, shape, spread, most, shards=(), kind=jnp.bfloat16):
    values = spread * jax.random.normal(own_key, shape, jnp.float32)
    if shards:
        values = values * block_scale(own_key, shape, shards, -0.22, 0.18)
    return jnp.clip(values, -most, most).astype(kind)


def setup_inputs(seed: int = 0) -> dict:
    streams_of = jax.random.split(jax.random.key(seed), 8)
    queries = draw_queries(jax.random.fold_in(streams_of[7], 71), 0)
    prefix_cache = draw_prefix_cache(jax.random.fold_in(streams_of[7], 71), 0)
    suffix_cache = draw_suffix_cache(jax.random.fold_in(streams_of[7], 71), 0)
    suffix_lengths = draw_suffix_lengths(jax.random.fold_in(streams_of[7], 71), 0)
    request_prefix_keys = jax.random.split(jax.random.fold_in(streams_of[4], 1), REQUESTS // REQ_DEV)
    request_prefix_turns = jax.random.permutation(jax.random.fold_in(streams_of[4], 3), REQUESTS // REQ_DEV)
    request_prefix = jax.vmap(lambda own, number: deal_out(jax.random.fold_in(streams_of[4], 2), own, number, REQ_DEV, PREFIXES, 1, CAP, 2))(request_prefix_keys, request_prefix_turns).reshape((REQUESTS, 1))
    prefix_owner = jax.random.permutation(streams_of[5], PREFIXES).astype(jnp.int32)
    out_proj = scatter_about(streams_of[6], (HEADS * HD, WIDTH), (HEADS * HD // 8) ** -0.5, 0.25, ((0, 8),))
    return {"queries": queries, "prefix_cache": prefix_cache, "suffix_cache": suffix_cache, "suffix_lengths": suffix_lengths, "request_prefix": request_prefix, "prefix_owner": prefix_owner, "out_proj": out_proj}


def softmax_partial(scores, value_rows, usable):
    if usable is not None:
        scores = jnp.where(usable, scores, -jnp.inf)
    highest = lax.optimization_barrier(jnp.max(scores, axis=-1, keepdims=True))
    weight = jnp.exp(scores - highest)
    weight_sum = lax.optimization_barrier(jnp.sum(weight, axis=-1))
    rounded = lax.optimization_barrier(weight.astype(jnp.bfloat16)).astype(jnp.float32)
    numer = jnp.einsum('rsvgl,rvdl->rsvgd', rounded, value_rows)
    return (numer / weight_sum[..., None], highest[..., 0] + jnp.log(weight_sum))

def reference(queries, prefix_cache, suffix_cache, suffix_lengths, request_prefix, prefix_owner, out_proj):
    group_size = HEADS // KVH
    scale = 1.0 / math.sqrt(HD)
    owner_slot = prefix_owner[request_prefix[:, 0]].astype(jnp.int32)
    block_size = 16
    block_count = REQUESTS // block_size

    def one_block(inputs):
        query_rows, slots, suffix_rows, lengths = inputs
        query_full = query_rows.astype(jnp.float32).reshape(block_size, STEPS, KVH, group_size, HD)
        prefix_rows = prefix_cache[slots].astype(jnp.float32)
        prefix_scores = jnp.einsum('rsvgd,rvdl->rsvgl', query_full, prefix_rows[:, :, :HD, :]) * scale
        prefix_out, prefix_lse = softmax_partial(prefix_scores, prefix_rows[:, :, HD:, :], None)
        suffix_full = suffix_rows.astype(jnp.float32)
        suffix_scores = jnp.einsum('rsvgd,rvdl->rsvgl', query_full, suffix_full[:, :, :HD, :]) * scale
        positions = jnp.arange(SUF, dtype=jnp.int32)
        limits = lengths[:, None] - (STEPS - 1) + jnp.arange(STEPS, dtype=jnp.int32)[None, :]
        usable = positions[None, None, None, None, :] < limits[:, :, None, None, None]
        suffix_out, suffix_lse = softmax_partial(suffix_scores, suffix_full[:, :, HD:, :], usable)
        total_lse = jnp.logaddexp(prefix_lse, suffix_lse)
        attention = prefix_out * jnp.exp(prefix_lse - total_lse)[..., None] + suffix_out * jnp.exp(suffix_lse - total_lse)[..., None]
        return attention.astype(jnp.bfloat16).reshape(block_size, STEPS, HEADS * HD)
    attention = lax.map(one_block, (queries.reshape(block_count, block_size, STEPS, HEADS * HD), owner_slot.reshape(block_count, block_size), suffix_cache.reshape(block_count, block_size, KVH, 2 * HD, SUF), suffix_lengths.reshape(block_count, block_size)))
    attention = attention.reshape(REQUESTS * STEPS, HEADS * HD)
    slice_width = HEADS * HD // N_TENSOR
    summed = jnp.zeros((REQUESTS * STEPS, WIDTH), jnp.float32)
    for index in range(N_TENSOR):
        left = attention[:, index * slice_width:(index + 1) * slice_width].astype(jnp.float32)
        right = out_proj[index * slice_width:(index + 1) * slice_width].astype(jnp.float32)
        group_part = jnp.dot(left, right, precision=lax.Precision.HIGHEST, preferred_element_type=jnp.float32)
        group_part = lax.optimization_barrier(group_part.astype(jnp.bfloat16)).astype(jnp.float32)
        summed = summed + group_part
    return summed.astype(jnp.bfloat16).reshape(REQUESTS, STEPS, WIDTH)
```

```python
import functools

import jax
import jax.numpy as jnp
from jax import lax
from jax.experimental import pallas as pl
from jax.experimental.pallas import tpu as pltpu
from jax.sharding import PartitionSpec as P

LANES = 128
HALF = 64
X_SIZE = 4
CAPACITY = 2
GROUPS = X_SIZE * CAPACITY
STEPS = 3
ROWS = 12
PAD_ROWS = 16
SCALE = 0.125
VMEM_LIMIT = 56 * 1024 * 1024


def lane_iota(rows):
    return lax.broadcasted_iota(jnp.int32, (rows, LANES), 1)


def split_heads(rows):
    low = lane_iota(rows.shape[0]) < HALF
    even = jnp.where(low, rows, 0.0)
    odd = jnp.where(low, pltpu.roll(rows, HALF, 1), 0.0)
    return even, odd


def join_heads(even, odd):
    low = lane_iota(even.shape[0]) < HALF
    return jnp.where(low, pltpu.roll(even, HALF, 1), odd)


def nt_dot(left, right):
    return lax.dot_general(
        left, right, (((1,), (1,)), ((), ())), preferred_element_type=jnp.float32
    )


def route_kernel(me_ref, prefix_ref, owner_ref, q_ref, send_ref, rows_ref, code_ref, taken, source, qs, acc):
    requests = q_ref.shape[1]
    z_size = send_ref.shape[0]
    x_own = me_ref[0] % X_SIZE

    def clear(i, _):
        taken[i] = 0
        return 0

    lax.fori_loop(0, owner_ref.shape[0], clear, 0)

    def clear_source(i, _):
        source[i] = 0
        return 0

    lax.fori_loop(0, z_size * GROUPS, clear_source, 0)

    def place(r, _):
        name = prefix_ref[me_ref[0] * requests + r]
        owner = owner_ref[name]
        rank = taken[name]
        taken[name] = rank + 1
        offset = (owner % X_SIZE - x_own + X_SIZE) % X_SIZE
        code = (owner // X_SIZE) * GROUPS + offset * CAPACITY + rank
        code_ref[r] = code
        source[code] = r
        return 0

    lax.fori_loop(0, requests, place, 0)
    zeros = jnp.zeros((requests, LANES), jnp.float32)
    for i in range(PAD_ROWS):
        if i < ROWS:
            step, pair = divmod(i, ROWS // STEPS)
            value = q_ref[step, :, pair * LANES : (pair + 1) * LANES].astype(jnp.float32)
        else:
            value = zeros
        qs[pl.ds(i, requests, stride=PAD_ROWS), :] = value
    rows_ref[...] = qs[...].astype(jnp.bfloat16)

    def fill(z, _):
        for slot in range(GROUPS):
            r = source[z * GROUPS + slot]
            block = qs[pl.ds(pl.multiple_of(r * PAD_ROWS, PAD_ROWS), PAD_ROWS), :]
            acc[slot * ROWS : (slot + 1) * ROWS, :] = block[:ROWS]
        send_ref[z] = acc[...].astype(jnp.bfloat16)
        return 0

    lax.fori_loop(0, z_size, fill, 0)


def route(me, prefixes, owner, q3, z_size):
    requests = q3.shape[1]
    smem = pl.BlockSpec(memory_space=pltpu.SMEM)
    vmem = pl.BlockSpec(memory_space=pltpu.VMEM)
    return pl.pallas_call(
        route_kernel,
        out_shape=(
            jax.ShapeDtypeStruct((z_size, GROUPS * ROWS, LANES), jnp.bfloat16),
            jax.ShapeDtypeStruct((requests * PAD_ROWS, LANES), jnp.bfloat16),
            jax.ShapeDtypeStruct((requests,), jnp.int32),
        ),
        in_specs=[smem, smem, smem, vmem],
        out_specs=(vmem, vmem, smem),
        scratch_shapes=[
            pltpu.SMEM((owner.shape[0],), jnp.int32),
            pltpu.SMEM((z_size * GROUPS,), jnp.int32),
            pltpu.VMEM((requests * PAD_ROWS, LANES), jnp.float32),
            pltpu.VMEM((GROUPS * ROWS, LANES), jnp.float32),
        ],
        compiler_params=pltpu.CompilerParams(vmem_limit_bytes=VMEM_LIMIT),
        name="route",
    )(me, prefixes, owner, q3)


SUFFIX_BLOCK = 8


def suffix_kernel(length_ref, q_ref, kv_ref, out_ref, lse_ref):
    base = pl.program_id(0) * SUFFIX_BLOCK
    positions = kv_ref.shape[1]
    shape = (2 * PAD_ROWS, positions)
    step = lax.broadcasted_iota(jnp.int32, shape, 0) % PAD_ROWS // (ROWS // STEPS)
    past = lax.broadcasted_iota(jnp.int32, shape, 1) - step
    low = lane_iota(PAD_ROWS) < HALF
    for r in range(SUFFIX_BLOCK):
        rows = slice(r * PAD_ROWS, (r + 1) * PAD_ROWS)
        even, odd = split_heads(q_ref[rows].astype(jnp.float32) * SCALE)
        query = jnp.concatenate([even, odd], axis=0).astype(jnp.bfloat16)
        cache = kv_ref[r]
        scores = nt_dot(query, cache)
        usable = past < length_ref[base + r] - (STEPS - 1)
        scores = jnp.where(usable, scores, -jnp.inf)
        highest = jnp.max(scores, axis=1, keepdims=True)
        weight = jnp.exp(scores - highest)
        total = jnp.sum(weight, axis=1, keepdims=True)
        mixed = jnp.dot(weight.astype(jnp.bfloat16), cache, preferred_element_type=jnp.float32)
        mixed = mixed / total
        lse = highest + jnp.log(total)
        out_ref[rows] = join_heads(mixed[:PAD_ROWS], mixed[PAD_ROWS:])
        lse_ref[rows] = jnp.where(low, lse[:PAD_ROWS], lse[PAD_ROWS:])


def suffix_attention(lengths, q_rows, kv):
    requests, positions, _ = kv.shape
    block = SUFFIX_BLOCK * PAD_ROWS
    row_spec = pl.BlockSpec((block, LANES), lambda i: (i, 0))
    shape = jax.ShapeDtypeStruct((requests * PAD_ROWS, LANES), jnp.float32)
    return pl.pallas_call(
        suffix_kernel,
        grid=(requests // SUFFIX_BLOCK,),
        out_shape=(shape, shape),
        in_specs=[
            pl.BlockSpec(memory_space=pltpu.SMEM),
            row_spec,
            pl.BlockSpec((SUFFIX_BLOCK, positions, LANES), lambda i: (i, 0, 0)),
        ],
        out_specs=(row_spec, row_spec),
        compiler_params=pltpu.CompilerParams(vmem_limit_bytes=VMEM_LIMIT),
        cost_estimate=pl.CostEstimate(
            flops=4 * requests * 32 * 128 * 80 * 8, bytes_accessed=8_000_000, transcendentals=0
        ),
        name="suffix",
    )(lengths, q_rows, kv)


SOURCE_BLOCK = 8
PIECES = 3


def prefix_kernel(me_ref, recv_ref, kv_ref, ret_ref, cache, queries, acc):
    group, block = pl.program_id(0), pl.program_id(1)
    span = CAPACITY * ROWS
    rows = SOURCE_BLOCK * span

    @pl.when(jnp.logical_and(group == 0, block == 0))
    def _():
        queries[...] = recv_ref[...].astype(jnp.float32) * SCALE
        cache[LANES:, :] = jnp.ones_like(cache[LANES:, :])

    @pl.when(block == 0)
    def _():
        cache[:LANES, :] = kv_ref[0]

    sources = pl.ds(block * SOURCE_BLOCK, SOURCE_BLOCK)
    place = pl.ds(pl.multiple_of(group * span, 8), span)
    both = split_heads(queries[sources, place, :].reshape(rows, LANES))
    results = []
    for query in both:
        scores = jnp.dot(
            query.astype(jnp.bfloat16), cache[:LANES, :], preferred_element_type=jnp.float32
        )
        highest = jnp.max(scores, axis=1, keepdims=True)
        weight = jnp.exp(scores - highest).astype(jnp.bfloat16)
        mixed = nt_dot(weight, cache[...])
        total = mixed[:, LANES:]
        results.append((mixed[:, :LANES] / total, highest + jnp.log(total)))
    low = lane_iota(rows) < HALF
    acc[sources, place, :] = join_heads(results[0][0], results[1][0]).reshape(
        SOURCE_BLOCK, span, LANES
    )
    lse = jnp.where(low, results[0][1], results[1][1])
    high_part = lse.astype(jnp.bfloat16)
    rest = lse - high_part.astype(jnp.float32)
    mid_part = rest.astype(jnp.bfloat16)
    low_part = (rest - mid_part.astype(jnp.float32)).astype(jnp.bfloat16)
    lane = lane_iota(rows) % HALF
    row = lax.broadcasted_iota(jnp.int32, (rows, LANES), 0) % ROWS
    packed = jnp.zeros((rows, LANES), jnp.float32)
    for i, part in enumerate((high_part, mid_part, low_part)):
        packed = jnp.where(lane == row + i * ROWS, part.astype(jnp.float32), packed)
    slots = SOURCE_BLOCK * CAPACITY
    pick = lax.broadcasted_iota(jnp.int32, (slots, rows), 1) // ROWS
    pick = (pick == lax.broadcasted_iota(jnp.int32, (slots, rows), 0)).astype(jnp.bfloat16)
    lse_rows = jnp.dot(pick, packed.astype(jnp.bfloat16), preferred_element_type=jnp.float32)
    for g in range(X_SIZE):

        @pl.when(group == g)
        def _():
            for source in range(SOURCE_BLOCK):
                acc[block * SOURCE_BLOCK + source, GROUPS * ROWS + g * CAPACITY : GROUPS * ROWS + (g + 1) * CAPACITY, :] = (
                    lse_rows[source * CAPACITY : (source + 1) * CAPACITY]
                )

    last = jnp.logical_and(group == pl.num_programs(0) - 1, block == pl.num_programs(1) - 1)

    @pl.when(last)
    def _():
        ret_ref[...] = acc[...].astype(jnp.bfloat16)


def prefix_attention(me, recv, kv):
    z_size = recv.shape[0]
    length = kv.shape[2]
    whole = lambda *shape: pl.BlockSpec(shape, lambda g, b, me: (0,) * len(shape))
    out_rows = GROUPS * ROWS + GROUPS
    return pl.pallas_call(
        prefix_kernel,
        out_shape=jax.ShapeDtypeStruct((z_size, out_rows, LANES), jnp.bfloat16),
        grid_spec=pltpu.PrefetchScalarGridSpec(
            num_scalar_prefetch=1,
            grid=(X_SIZE, z_size // SOURCE_BLOCK),
            in_specs=[
                whole(*recv.shape),
                pl.BlockSpec((1, LANES, length), lambda g, b, me: ((me[0] + g) % X_SIZE, 0, 0)),
            ],
            out_specs=whole(z_size, out_rows, LANES),
            scratch_shapes=[
                pltpu.VMEM((2 * LANES, length), jnp.bfloat16),
                pltpu.VMEM(recv.shape, jnp.float32),
                pltpu.VMEM((z_size, out_rows, LANES), jnp.float32),
            ],
        ),
        compiler_params=pltpu.CompilerParams(vmem_limit_bytes=VMEM_LIMIT),
        cost_estimate=pl.CostEstimate(
            flops=8_000_000_000, bytes_accessed=4_000_000, transcendentals=0
        ),
        name="prefix",
    )(me, recv, kv)


def merge_kernel(code_ref, ret_ref, suffix_ref, suffix_lse_ref, w_ref, out_ref, spread, picked, merged, left):
    z_size = ret_ref.shape[0]
    requests = code_ref.shape[0]
    slot_rows = GROUPS * PAD_ROWS

    @pl.when(pl.program_id(0) == 0)
    def _():
        for z in range(z_size):
            block = ret_ref[z].astype(jnp.float32)
            for slot in range(GROUPS):
                spread[z, slot * PAD_ROWS : slot * PAD_ROWS + ROWS, :] = block[slot * ROWS : (slot + 1) * ROWS]
                spread[z, slot * PAD_ROWS + ROWS : slot * PAD_ROWS + ROWS + 1, :] = block[
                    GROUPS * ROWS + slot : GROUPS * ROWS + slot + 1
                ]

        def pick(r, _):
            code = code_ref[r]
            start = pl.multiple_of(code % GROUPS * PAD_ROWS, PAD_ROWS)
            picked[pl.ds(pl.multiple_of(r * PAD_ROWS, PAD_ROWS), PAD_ROWS), :] = spread[
                code // GROUPS, pl.ds(start, PAD_ROWS), :
            ]
            return 0

        lax.fori_loop(0, requests, pick, 0, unroll=8)
        total_rows = requests * PAD_ROWS
        packed = picked[pl.ds(ROWS, requests, stride=PAD_ROWS), :].astype(jnp.bfloat16)
        owner = lax.broadcasted_iota(jnp.int32, (total_rows, requests), 0) // PAD_ROWS
        owner = owner == lax.broadcasted_iota(jnp.int32, (total_rows, requests), 1)
        copies = jnp.dot(owner.astype(jnp.bfloat16), packed, preferred_element_type=jnp.float32)
        lane = lane_iota(total_rows) % HALF
        row = lax.broadcasted_iota(jnp.int32, (total_rows, LANES), 0) % PAD_ROWS
        own = jnp.logical_and(lane < PIECES * ROWS, lane % ROWS == row)
        copies = jnp.where(own, copies, 0.0).astype(jnp.bfloat16)
        same_half = lax.broadcasted_iota(jnp.int32, (LANES, LANES), 0) // HALF
        same_half = same_half == lane_iota(LANES) // HALF
        prefix_lse = jnp.dot(copies, same_half.astype(jnp.bfloat16), preferred_element_type=jnp.float32)
        gap = prefix_lse - suffix_lse_ref[...]
        small = jnp.exp(-jnp.abs(gap))
        large_weight = 1.0 / (1.0 + small)
        small_weight = small * large_weight
        prefix_first = gap >= 0.0
        merged[...] = picked[...] * jnp.where(prefix_first, large_weight, small_weight) + suffix_ref[
            ...
        ] * jnp.where(prefix_first, small_weight, large_weight)
        pairs = ROWS // STEPS
        for step in range(STEPS):
            for pair in range(pairs):
                left[step * requests : (step + 1) * requests, pair * LANES : (pair + 1) * LANES] = merged[
                    pl.ds(step * pairs + pair, requests, stride=PAD_ROWS), :
                ].astype(jnp.bfloat16)

    out_ref[0] = nt_dot(left[...], w_ref[0]).astype(jnp.bfloat16)


def merge_project(codes, ret, suffix_out, suffix_lse, weights, parts):
    requests = codes.shape[0]
    width = weights.shape[0] // parts
    depth = weights.shape[1]
    total_rows = requests * PAD_ROWS
    whole = lambda array: pl.BlockSpec(array.shape, lambda t: (0,) * array.ndim)
    return pl.pallas_call(
        merge_kernel,
        grid=(parts,),
        out_shape=jax.ShapeDtypeStruct((parts, STEPS * requests, width), jnp.bfloat16),
        in_specs=[
            pl.BlockSpec(memory_space=pltpu.SMEM),
            whole(ret),
            whole(suffix_out),
            whole(suffix_lse),
            pl.BlockSpec((1, width, depth), lambda t: (t, 0, 0)),
        ],
        out_specs=pl.BlockSpec((1, STEPS * requests, width), lambda t: (t, 0, 0)),
        scratch_shapes=[
            pltpu.VMEM((ret.shape[0], GROUPS * PAD_ROWS, LANES), jnp.float32),
            pltpu.VMEM((total_rows, LANES), jnp.float32),
            pltpu.VMEM((total_rows, LANES), jnp.float32),
            pltpu.VMEM((STEPS * requests, depth), jnp.bfloat16),
        ],
        compiler_params=pltpu.CompilerParams(vmem_limit_bytes=VMEM_LIMIT),
        name="merge",
    )(codes, ret, suffix_out, suffix_lse, weights.reshape(parts, width, depth))


def shards(queries, prefix_cache, suffix_cache, suffix_lengths, request_prefix, prefix_owner, out_proj):
    prefix_size = lax.axis_size("prefix")
    tensor_size = lax.axis_size("tensor")
    z_size = prefix_size // X_SIZE
    x_groups = [[z * X_SIZE + x for x in range(X_SIZE)] for z in range(z_size)]
    z_groups = [[z * X_SIZE + x for z in range(z_size)] for x in range(X_SIZE)]
    me = lax.axis_index("prefix").astype(jnp.int32).reshape(1)
    kv = lax.all_gather(prefix_cache[0, 0], "prefix", axis=0, axis_index_groups=x_groups)
    q3 = queries.transpose(1, 0, 2)
    send, q_rows, codes = route(me, request_prefix.reshape(-1), prefix_owner, q3, z_size)
    recv = lax.all_to_all(
        send, "prefix", split_axis=0, concat_axis=0, axis_index_groups=z_groups, tiled=True
    )
    suffix_rows = suffix_cache[:, 0].transpose(0, 2, 1)
    suffix_out, suffix_lse = suffix_attention(suffix_lengths, q_rows, suffix_rows)
    ret = prefix_attention(me, recv, kv)
    homed = lax.all_to_all(
        ret, "prefix", split_axis=0, concat_axis=0, axis_index_groups=z_groups, tiled=True
    )
    parts = merge_project(codes, homed, suffix_out, suffix_lse, out_proj.T, tensor_size)
    parts = lax.all_to_all(parts, "tensor", split_axis=0, concat_axis=0, tiled=True)
    summed = jnp.sum(parts.astype(jnp.float32), axis=0).astype(jnp.bfloat16)
    return summed.reshape(STEPS, queries.shape[0], -1).transpose(1, 0, 2)


def solution(mesh):
    return jax.shard_map(
        shards,
        mesh=mesh,
        in_specs=(
            P("prefix", None, "tensor"),
            P("prefix", "tensor", None, None),
            P("prefix", "tensor", None, None),
            P("prefix"),
            P(),
            P(),
            P("tensor", None),
        ),
        out_specs=P("prefix", None, "tensor"),
        check_vma=False,
    )
```

```python
import functools

import jax
import jax.numpy as jnp
from jax import lax
from jax.experimental import pallas as pl
from jax.experimental.pallas import tpu as pltpu
from jax.sharding import PartitionSpec as P

LANES = 128
HALF = 64
X_SIZE = 4
CORES = 2
CAPACITY = 2
GROUPS = X_SIZE * CAPACITY
STEPS = 3
ROWS = 12
PAD_ROWS = 16
SCALE = 0.125
VMEM_LIMIT = 56 * 1024 * 1024


def lane_iota(rows):
    return lax.broadcasted_iota(jnp.int32, (rows, LANES), 1)


def split_heads(rows):
    low = lane_iota(rows.shape[0]) < HALF
    even = jnp.where(low, rows, 0.0)
    odd = jnp.where(low, pltpu.roll(rows, HALF, 1), 0.0)
    return even, odd


def join_heads(even, odd):
    low = lane_iota(even.shape[0]) < HALF
    return jnp.where(low, pltpu.roll(even, HALF, 1), odd)


def nt_dot(left, right):
    return lax.dot_general(
        left, right, (((1,), (1,)), ((), ())), preferred_element_type=jnp.float32
    )


def spread_queries(q_ref, qs):
    requests = q_ref.shape[1]
    for i in range(PAD_ROWS):
        if i < ROWS:
            step, pair = divmod(i, ROWS // STEPS)
            value = q_ref[step, :, pair * LANES : (pair + 1) * LANES].astype(jnp.float32)
        else:
            value = jnp.zeros((requests, LANES), jnp.float32)
        qs[pl.ds(i, requests, stride=PAD_ROWS), :] = value


def route_kernel(me_ref, prefix_ref, owner_ref, q_ref, send_ref, code_ref, taken, source, qs, acc):
    requests = q_ref.shape[1]
    z_size = send_ref.shape[0]
    me = me_ref[0]
    x_own = me & (X_SIZE - 1)
    for i in range(owner_ref.shape[0]):
        taken[i] = 0
    for i in range(z_size * GROUPS):
        source[i] = 0

    def place(r, _):
        name = prefix_ref[me * requests + r]
        owner = owner_ref[name]
        rank = taken[name]
        taken[name] = rank + 1
        offset = (owner - x_own) & (X_SIZE - 1)
        code = (owner >> 2) * GROUPS + offset * CAPACITY + rank
        code_ref[r] = code
        source[code] = r
        return 0

    lax.fori_loop(0, requests, place, 0, unroll=8)
    spread_queries(q_ref, qs)

    def fill(z, _):
        for slot in range(GROUPS):
            r = source[z * GROUPS + slot]
            block = qs[pl.ds(pl.multiple_of(r * PAD_ROWS, PAD_ROWS), PAD_ROWS), :]
            acc[z, slot * ROWS : (slot + 1) * ROWS, :] = block[:ROWS]
        return 0

    lax.fori_loop(0, z_size, fill, 0, unroll=4)
    send_ref[...] = acc[...].astype(jnp.bfloat16)


def route(me, prefixes, owner, q3, z_size):
    requests = q3.shape[1]
    smem = pl.BlockSpec(memory_space=pltpu.SMEM)
    vmem = pl.BlockSpec(memory_space=pltpu.VMEM)
    shape = (z_size, GROUPS * ROWS, LANES)
    return pl.pallas_call(
        route_kernel,
        out_shape=(
            jax.ShapeDtypeStruct(shape, jnp.bfloat16),
            jax.ShapeDtypeStruct((requests,), jnp.int32),
        ),
        in_specs=[smem, smem, smem, vmem],
        out_specs=(vmem, smem),
        scratch_shapes=[
            pltpu.SMEM((owner.shape[0],), jnp.int32),
            pltpu.SMEM((z_size * GROUPS,), jnp.int32),
            pltpu.VMEM((requests * PAD_ROWS, LANES), jnp.float32),
            pltpu.VMEM(shape, jnp.float32),
        ],
        compiler_params=pltpu.CompilerParams(vmem_limit_bytes=VMEM_LIMIT),
        name="route",
    )(me, prefixes, owner, q3)


SUFFIX_BLOCK = 4


def suffix_kernel(length_ref, q_ref, kv_ref, out_ref, lse_ref, qs):
    spread_queries(q_ref, qs)
    requests, positions, _ = kv_ref.shape
    rows = SUFFIX_BLOCK * PAD_ROWS
    shape = (2 * rows, SUFFIX_BLOCK * positions)
    row = lax.broadcasted_iota(jnp.int32, shape, 0) % rows
    request = row // PAD_ROWS
    step = row % PAD_ROWS // (ROWS // STEPS)
    place = lax.broadcasted_iota(jnp.int32, shape, 1) - request * positions
    past = jnp.where(place >= 0, place - step, 2 * positions)
    request_rows = lax.broadcasted_iota(jnp.int32, (2 * rows, 1), 0) % rows // PAD_ROWS
    low = lane_iota(rows) < HALF

    def some(i, _):
        here = pl.ds(pl.multiple_of(i * rows, rows), rows)
        even, odd = split_heads(qs[here, :] * SCALE)
        query = jnp.concatenate([even, odd], axis=0).astype(jnp.bfloat16)
        cache = kv_ref[pl.ds(i * SUFFIX_BLOCK, SUFFIX_BLOCK)].reshape(-1, LANES)
        limit = jnp.zeros((2 * rows, 1), jnp.int32)
        for r in range(SUFFIX_BLOCK):
            limit = jnp.where(request_rows == r, length_ref[i * SUFFIX_BLOCK + r] - (STEPS - 1), limit)
        scores = jnp.where(past < limit, nt_dot(query, cache), -jnp.inf)
        highest = jnp.max(scores, axis=1, keepdims=True)
        weight = jnp.exp(scores - highest)
        total = jnp.sum(weight, axis=1, keepdims=True)
        mixed = jnp.dot(weight.astype(jnp.bfloat16), cache, preferred_element_type=jnp.float32)
        mixed = mixed / total
        lse = highest + jnp.log(total)
        out_ref[here, :] = join_heads(mixed[:rows], mixed[rows:])
        lse_ref[here, :] = jnp.where(low, lse[:rows], lse[rows:])
        return 0

    lax.fori_loop(0, requests // SUFFIX_BLOCK, some, 0, unroll=2)


def suffix_attention(lengths, q3, kv):
    requests = kv.shape[0]
    vmem = pl.BlockSpec(memory_space=pltpu.VMEM)
    shape = jax.ShapeDtypeStruct((requests * PAD_ROWS, LANES), jnp.float32)
    return pl.pallas_call(
        suffix_kernel,
        out_shape=(shape, shape),
        in_specs=[pl.BlockSpec(memory_space=pltpu.SMEM), vmem, vmem],
        out_specs=(vmem, vmem),
        scratch_shapes=[pltpu.VMEM((requests * PAD_ROWS, LANES), jnp.float32)],
        compiler_params=pltpu.CompilerParams(vmem_limit_bytes=VMEM_LIMIT),
        cost_estimate=pl.CostEstimate(
            flops=8_000_000_000, bytes_accessed=8_000_000, transcendentals=0
        ),
        name="suffix",
    )(lengths, q3, kv)


CHUNKS = 2


def prefix_kernel(me_ref, recv_ref, kv_ref, ret_ref, values, queries, acc):
    group = pl.program_id(0)
    z_size = recv_ref.shape[0]
    span = CAPACITY * ROWS
    rows = z_size * span

    @pl.when(group == 0)
    def _():
        queries[...] = recv_ref[...].astype(jnp.float32) * SCALE
        values[HALF:, :] = jnp.ones_like(values[HALF:, :])

    values[:HALF, :] = kv_ref[0, HALF:]
    place = pl.ds(pl.multiple_of(group * span, 8), span)
    query = jnp.concatenate(split_heads(queries[:, place, :].reshape(rows, LANES)), axis=0)
    query = query.astype(jnp.bfloat16)
    size = 2 * rows // CHUNKS
    scores, weights, mixes = [None] * CHUNKS, [None] * CHUNKS, []
    for stage in range(CHUNKS + 2):
        if stage < CHUNKS:
            here = query[stage * size : (stage + 1) * size]
            scores[stage] = jnp.dot(here, kv_ref[0], preferred_element_type=jnp.float32)
        if stage >= 2:
            weight, highest = weights[stage - 2]
            mixed = nt_dot(weight, values[...])
            low = lane_iota(size) < HALF
            total = jnp.where(low, pltpu.roll(mixed, HALF, 1), mixed)
            mixes.append((mixed / total, highest + jnp.log(total)))
        if 1 <= stage <= CHUNKS:
            highest = jnp.max(scores[stage - 1], axis=1, keepdims=True)
            weight = jnp.exp(scores[stage - 1] - highest).astype(jnp.bfloat16)
            weights[stage - 1] = (weight, highest)
    half = CHUNKS // 2
    low = lane_iota(size) < HALF
    lse = []
    for i in range(half):
        out = jnp.where(low, mixes[i][0], pltpu.roll(mixes[i + half][0], HALF, 1))
        sources = slice(i * z_size // half, (i + 1) * z_size // half)
        acc[sources, place, :] = out.reshape(z_size // half, span, LANES)
        lse.append(jnp.where(low, mixes[i][1], mixes[i + half][1]))
    lse = jnp.concatenate(lse, axis=0)
    lane = lax.broadcasted_iota(jnp.int32, (span, LANES), 1) & (HALF - 1)
    row = lax.broadcasted_iota(jnp.int32, (span, LANES), 0)
    row = jnp.where(row < ROWS, row, row - ROWS)
    high_part = lse.astype(jnp.bfloat16).astype(jnp.float32)
    rest = lse - high_part
    mid_part = rest.astype(jnp.bfloat16).astype(jnp.float32)
    packed = jnp.zeros((z_size, span, LANES), jnp.float32)
    for i, part in enumerate((high_part, mid_part, rest - mid_part)):
        part = part.reshape(z_size, span, LANES)
        packed = jnp.where((lane == row + i * ROWS)[None], part, packed)
    packed = packed.reshape(rows, LANES).astype(jnp.bfloat16)
    shape = (z_size * GROUPS, rows)
    slot = lax.broadcasted_iota(jnp.int32, shape, 0)
    inside = (slot & (GROUPS - 1)) // CAPACITY == group
    slot = slot // GROUPS * CAPACITY + (slot & (CAPACITY - 1))
    first = lax.broadcasted_iota(jnp.int32, shape, 1) - slot * ROWS
    pick = jnp.logical_and(inside, jnp.logical_and(first >= 0, first < ROWS))
    lse_rows = jnp.dot(pick.astype(jnp.bfloat16), packed, preferred_element_type=jnp.float32)
    lse_rows = lse_rows.reshape(z_size, GROUPS, LANES)
    own = lax.broadcasted_iota(jnp.int32, (GROUPS, LANES), 0) // CAPACITY == group
    acc[:, GROUPS * ROWS :, :] = jnp.where(own[None], lse_rows, acc[:, GROUPS * ROWS :, :])

    @pl.when(group == pl.num_programs(0) - 1)
    def _():
        ret_ref[...] = acc[...].astype(jnp.bfloat16)


def prefix_attention(me, recv, kv):
    z_size = recv.shape[0]
    length = kv.shape[2]
    whole = lambda *shape: pl.BlockSpec(shape, lambda g, me: (0,) * len(shape))
    out_rows = GROUPS * ROWS + GROUPS
    return pl.pallas_call(
        prefix_kernel,
        out_shape=jax.ShapeDtypeStruct((z_size, out_rows, LANES), jnp.bfloat16),
        grid_spec=pltpu.PrefetchScalarGridSpec(
            num_scalar_prefetch=1,
            grid=(X_SIZE,),
            in_specs=[
                whole(*recv.shape),
                pl.BlockSpec((1, LANES, length), lambda g, me: ((me[0] + g) % X_SIZE, 0, 0)),
            ],
            out_specs=whole(z_size, out_rows, LANES),
            scratch_shapes=[
                pltpu.VMEM((LANES, length), jnp.bfloat16),
                pltpu.VMEM(recv.shape, jnp.float32),
                pltpu.VMEM((z_size, out_rows, LANES), jnp.float32),
            ],
        ),
        compiler_params=pltpu.CompilerParams(vmem_limit_bytes=VMEM_LIMIT),
        cost_estimate=pl.CostEstimate(
            flops=8_000_000_000, bytes_accessed=4_000_000, transcendentals=0
        ),
        name="prefix",
    )(me, recv, kv)


def merge_kernel(code_ref, ret_ref, suffix_ref, suffix_lse_ref, w_ref, out_ref, wide, picked, packed, merged, left):
    requests = code_ref.shape[0]

    @pl.when(pl.program_id(0) == 0)
    def _():
        wide[...] = ret_ref[...].astype(jnp.float32)
        pair_rows = CAPACITY * ROWS
        for r in range(requests):
            code = code_ref[r]
            z, slot = code // GROUPS, code % GROUPS
            start = pl.multiple_of(slot // CAPACITY * pair_rows, 8)
            pair = wide[z, pl.ds(start, pair_rows), :]
            second = jnp.concatenate([pair[ROWS:], pair[: PAD_ROWS - ROWS]], axis=0)
            picked[r] = jnp.where(slot % CAPACITY == 0, pair[:PAD_ROWS], second)
            packed[r : r + 1, :] = wide[z, pl.ds(GROUPS * ROWS + slot, 1), :]
        lane = lane_iota(PAD_ROWS) % HALF
        row = lax.broadcasted_iota(jnp.int32, (PAD_ROWS, LANES), 0)
        own = jnp.logical_or(lane == row, jnp.logical_or(lane == row + ROWS, lane == row + 2 * ROWS))
        own = jnp.logical_and(own, row < ROWS)
        copies = jnp.where(own[None], packed[...][:, None, :], 0.0).astype(jnp.bfloat16)
        same_half = lax.broadcasted_iota(jnp.int32, (LANES, LANES), 0) // HALF
        same_half = same_half == lane_iota(LANES) // HALF
        prefix_lse = jnp.dot(
            copies.reshape(requests * PAD_ROWS, LANES),
            same_half.astype(jnp.bfloat16),
            preferred_element_type=jnp.float32,
        )
        gap = prefix_lse - suffix_lse_ref[...]
        small = jnp.exp(-jnp.abs(gap))
        large_weight = 1.0 / (1.0 + small)
        small_weight = small * large_weight
        prefix_first = gap >= 0.0
        merged[...] = picked[...].reshape(requests * PAD_ROWS, LANES) * jnp.where(
            prefix_first, large_weight, small_weight
        ) + suffix_ref[...] * jnp.where(prefix_first, small_weight, large_weight)
        pairs = ROWS // STEPS
        for step in range(STEPS):
            for pair in range(pairs):
                left[step * requests : (step + 1) * requests, pair * LANES : (pair + 1) * LANES] = merged[
                    pl.ds(step * pairs + pair, requests, stride=PAD_ROWS), :
                ].astype(jnp.bfloat16)

    for core in range(CORES):
        out_ref[core, 0] = nt_dot(left[...], w_ref[core]).astype(jnp.bfloat16)


def merge_project(codes, ret, suffix_out, suffix_lse, weights, parts):
    requests = codes.shape[0]
    width = weights.shape[0] // parts
    depth = weights.shape[1]
    whole = lambda array: pl.BlockSpec(array.shape, lambda t: (0,) * array.ndim)
    return pl.pallas_call(
        merge_kernel,
        grid=(parts // CORES,),
        out_shape=jax.ShapeDtypeStruct((CORES, parts // CORES, STEPS * requests, width), jnp.bfloat16),
        in_specs=[
            pl.BlockSpec(memory_space=pltpu.SMEM),
            whole(ret),
            whole(suffix_out),
            whole(suffix_lse),
            pl.BlockSpec((CORES, width, depth), lambda t: (t, 0, 0)),
        ],
        out_specs=pl.BlockSpec((CORES, 1, STEPS * requests, width), lambda t: (0, t, 0, 0)),
        scratch_shapes=[
            pltpu.VMEM(ret.shape, jnp.float32),
            pltpu.VMEM((requests, PAD_ROWS, LANES), jnp.float32),
            pltpu.VMEM((requests, LANES), jnp.float32),
            pltpu.VMEM((requests * PAD_ROWS, LANES), jnp.float32),
            pltpu.VMEM((STEPS * requests, depth), jnp.bfloat16),
        ],
        compiler_params=pltpu.CompilerParams(vmem_limit_bytes=VMEM_LIMIT),
        name="merge",
    )(codes, ret, suffix_out, suffix_lse, weights.reshape(parts, width, depth))


def shards(queries, prefix_cache, suffix_cache, suffix_lengths, request_prefix, prefix_owner, out_proj):
    prefix_size = lax.axis_size("prefix")
    tensor_size = lax.axis_size("tensor")
    z_size = prefix_size // X_SIZE
    x_groups = [[z * X_SIZE + x for x in range(X_SIZE)] for z in range(z_size)]
    z_groups = [[z * X_SIZE + x for z in range(z_size)] for x in range(X_SIZE)]
    me = lax.axis_index("prefix").astype(jnp.int32).reshape(1)
    kv = lax.all_gather(prefix_cache[0, 0], "prefix", axis=0, axis_index_groups=x_groups)
    q3 = queries.transpose(1, 0, 2)
    send, codes = route(me, request_prefix.reshape(-1), prefix_owner, q3, z_size)
    recv = lax.all_to_all(
        send, "prefix", split_axis=0, concat_axis=0, axis_index_groups=z_groups, tiled=True
    )
    suffix_rows = suffix_cache[:, 0].transpose(0, 2, 1)
    suffix_out, suffix_lse = suffix_attention(suffix_lengths, q3, suffix_rows)
    recv, suffix_out, suffix_lse = lax.optimization_barrier((recv, suffix_out, suffix_lse))
    ret = prefix_attention(me, recv, kv)
    homed = lax.all_to_all(
        ret, "prefix", split_axis=0, concat_axis=0, axis_index_groups=z_groups, tiled=True
    )
    parts = merge_project(codes, homed, suffix_out, suffix_lse, out_proj.T, tensor_size)
    y_size = tensor_size // CORES
    core_groups = [[y * CORES + c for c in range(CORES)] for y in range(y_size)]
    y_groups = [[y * CORES + c for y in range(y_size)] for c in range(CORES)]
    for groups in (core_groups, y_groups):
        parts = lax.all_to_all(
            parts, "tensor", split_axis=0, concat_axis=0, axis_index_groups=groups, tiled=True
        )
        parts = jnp.sum(parts.astype(jnp.float32), axis=0).astype(jnp.bfloat16)
    return parts.reshape(STEPS, queries.shape[0], -1).transpose(1, 0, 2)


def solution(mesh):
    return jax.shard_map(
        shards,
        mesh=mesh,
        in_specs=(
            P("prefix", None, "tensor"),
            P("prefix", "tensor", None, None),
            P("prefix", "tensor", None, None),
            P("prefix"),
            P(),
            P(),
            P("tensor", None),
        ),
        out_specs=P("prefix", None, "tensor"),
        check_vma=False,
    )
```

```python
import functools

import jax
import jax.numpy as jnp
from jax import lax
from jax.experimental import pallas as pl
from jax.experimental.pallas import tpu as pltpu
from jax.sharding import PartitionSpec as P

LANES = 128
HALF = 64
CORES = 2
CAPACITY = 2
STEPS = 3
ROWS = 12
PAD_ROWS = 16
SCALE = 0.125
VMEM_LIMIT = 56 * 1024 * 1024


def lane_iota(rows):
    return lax.broadcasted_iota(jnp.int32, (rows, LANES), 1)


def split_heads(rows):
    low = lane_iota(rows.shape[0]) < HALF
    even = jnp.where(low, rows, 0.0)
    odd = jnp.where(low, pltpu.roll(rows, HALF, 1), 0.0)
    return even, odd


def join_heads(even, odd):
    low = lane_iota(even.shape[0]) < HALF
    return jnp.where(low, pltpu.roll(even, HALF, 1), odd)


def nt_dot(left, right):
    return lax.dot_general(
        left, right, (((1,), (1,)), ((), ())), preferred_element_type=jnp.float32
    )


def spread_queries(q_ref, qs):
    requests = q_ref.shape[1]
    for i in range(PAD_ROWS):
        if i < ROWS:
            step, pair = divmod(i, ROWS // STEPS)
            value = q_ref[step, :, pair * LANES : (pair + 1) * LANES].astype(jnp.float32)
        else:
            value = jnp.zeros((requests, LANES), jnp.float32)
        qs[pl.ds(i, requests, stride=PAD_ROWS), :] = value


def route_kernel(me_ref, prefix_ref, owner_ref, q_ref, send_ref, code_ref, taken, source, qs, acc):
    requests = q_ref.shape[1]
    owners = send_ref.shape[0]
    me = me_ref[0]
    for i in range(owners):
        taken[i] = 0
    for i in range(owners * CAPACITY):
        source[i] = 0

    def place(r, _):
        name = prefix_ref[me * requests + r]
        rank = taken[name]
        taken[name] = rank + 1
        code = owner_ref[name] * CAPACITY + rank
        code_ref[r] = code
        source[code] = r
        return 0

    lax.fori_loop(0, requests, place, 0, unroll=8)
    spread_queries(q_ref, qs)

    def fill(owner, _):
        for rank in range(CAPACITY):
            r = source[owner * CAPACITY + rank]
            block = qs[pl.ds(pl.multiple_of(r * PAD_ROWS, PAD_ROWS), PAD_ROWS), :]
            acc[owner, rank * ROWS : (rank + 1) * ROWS, :] = block[:ROWS]
        return 0

    lax.fori_loop(0, owners, fill, 0, unroll=16)
    send_ref[...] = acc[...].astype(jnp.bfloat16)


def route(me, prefixes, owner, q3):
    requests = q3.shape[1]
    smem = pl.BlockSpec(memory_space=pltpu.SMEM)
    vmem = pl.BlockSpec(memory_space=pltpu.VMEM)
    shape = (owner.shape[0], CAPACITY * ROWS, LANES)
    return pl.pallas_call(
        route_kernel,
        out_shape=(
            jax.ShapeDtypeStruct(shape, jnp.bfloat16),
            jax.ShapeDtypeStruct((requests,), jnp.int32),
        ),
        in_specs=[smem, smem, smem, vmem],
        out_specs=(vmem, smem),
        scratch_shapes=[
            pltpu.SMEM((owner.shape[0],), jnp.int32),
            pltpu.SMEM((owner.shape[0] * CAPACITY,), jnp.int32),
            pltpu.VMEM((requests * PAD_ROWS, LANES), jnp.float32),
            pltpu.VMEM(shape, jnp.float32),
        ],
        compiler_params=pltpu.CompilerParams(vmem_limit_bytes=VMEM_LIMIT),
        name="route",
    )(me, prefixes, owner, q3)


SUFFIX_BLOCK = 4


def suffix_kernel(length_ref, q_ref, kv_ref, out_ref, lse_ref, qs):
    spread_queries(q_ref, qs)
    requests, positions, _ = kv_ref.shape
    rows = SUFFIX_BLOCK * PAD_ROWS
    shape = (2 * rows, SUFFIX_BLOCK * positions)
    row = lax.broadcasted_iota(jnp.int32, shape, 0) % rows
    request = row // PAD_ROWS
    step = row % PAD_ROWS // (ROWS // STEPS)
    place = lax.broadcasted_iota(jnp.int32, shape, 1) - request * positions
    past = jnp.where(place >= 0, place - step, 2 * positions)
    request_rows = lax.broadcasted_iota(jnp.int32, (2 * rows, 1), 0) % rows // PAD_ROWS
    low = lane_iota(rows) < HALF

    def some(i, _):
        here = pl.ds(pl.multiple_of(i * rows, rows), rows)
        even, odd = split_heads(qs[here, :] * SCALE)
        query = jnp.concatenate([even, odd], axis=0).astype(jnp.bfloat16)
        cache = kv_ref[pl.ds(i * SUFFIX_BLOCK, SUFFIX_BLOCK)].reshape(-1, LANES)
        limit = jnp.zeros((2 * rows, 1), jnp.int32)
        for r in range(SUFFIX_BLOCK):
            limit = jnp.where(request_rows == r, length_ref[i * SUFFIX_BLOCK + r] - (STEPS - 1), limit)
        scores = jnp.where(past < limit, nt_dot(query, cache), -jnp.inf)
        highest = jnp.max(scores, axis=1, keepdims=True)
        weight = jnp.exp(scores - highest)
        total = jnp.sum(weight, axis=1, keepdims=True)
        mixed = jnp.dot(weight.astype(jnp.bfloat16), cache, preferred_element_type=jnp.float32)
        mixed = mixed / total
        lse = highest + jnp.log(total)
        out_ref[here, :] = join_heads(mixed[:rows], mixed[rows:])
        lse_ref[here, :] = jnp.where(low, lse[:rows], lse[rows:])
        return 0

    lax.fori_loop(0, requests // SUFFIX_BLOCK, some, 0, unroll=2)


def suffix_attention(lengths, q3, kv):
    requests = kv.shape[0]
    vmem = pl.BlockSpec(memory_space=pltpu.VMEM)
    shape = jax.ShapeDtypeStruct((requests * PAD_ROWS, LANES), jnp.float32)
    return pl.pallas_call(
        suffix_kernel,
        out_shape=(shape, shape),
        in_specs=[pl.BlockSpec(memory_space=pltpu.SMEM), vmem, vmem],
        out_specs=(vmem, vmem),
        scratch_shapes=[pltpu.VMEM((requests * PAD_ROWS, LANES), jnp.float32)],
        compiler_params=pltpu.CompilerParams(vmem_limit_bytes=VMEM_LIMIT),
        cost_estimate=pl.CostEstimate(
            flops=8_000_000_000, bytes_accessed=8_000_000, transcendentals=0
        ),
        name="suffix",
    )(lengths, q3, kv)


SOURCES = 16
CHUNKS = 2


def prefix_kernel(recv_ref, kv_ref, ret_ref, values, acc):
    span = CAPACITY * ROWS
    rows = SOURCES * span

    @pl.when(pl.program_id(0) == 0)
    def _():
        values[:HALF, :] = kv_ref[HALF:]
        values[HALF:, :] = jnp.ones_like(values[HALF:, :])
        acc[...] = jnp.zeros_like(acc)

    received = recv_ref[...].astype(jnp.float32).reshape(rows, LANES) * SCALE
    query = jnp.concatenate(split_heads(received), axis=0).astype(jnp.bfloat16)
    size = 2 * rows // CHUNKS
    scores, weights, mixes = [None] * CHUNKS, [None] * CHUNKS, []
    for stage in range(CHUNKS + 2):
        if stage < CHUNKS:
            here = query[stage * size : (stage + 1) * size]
            scores[stage] = jnp.dot(here, kv_ref[...], preferred_element_type=jnp.float32)
        if stage >= 2:
            weight, highest = weights[stage - 2]
            mixed = nt_dot(weight, values[...])
            low = lane_iota(size) < HALF
            total = jnp.where(low, pltpu.roll(mixed, HALF, 1), mixed)
            mixes.append((mixed / total, highest + jnp.log(total)))
        if 1 <= stage <= CHUNKS:
            highest = jnp.max(scores[stage - 1], axis=1, keepdims=True)
            weight = jnp.exp(scores[stage - 1] - highest).astype(jnp.bfloat16)
            weights[stage - 1] = (weight, highest)
    out, lse = (jnp.concatenate([mix[i] for mix in mixes], axis=0) for i in range(2))
    low = lane_iota(rows) < HALF
    out = jnp.where(low, out[:rows], pltpu.roll(out[rows:], HALF, 1)).reshape(SOURCES, span, LANES)
    lse = jnp.where(low, lse[:rows], lse[rows:])
    lane = lax.broadcasted_iota(jnp.int32, (span, LANES), 1) & (HALF - 1)
    row = lax.broadcasted_iota(jnp.int32, (span, LANES), 0)
    row = jnp.where(row < ROWS, row, row - ROWS)
    high_part = lse.astype(jnp.bfloat16).astype(jnp.float32)
    rest = lse - high_part
    mid_part = rest.astype(jnp.bfloat16).astype(jnp.float32)
    packed = jnp.zeros((SOURCES, span, LANES), jnp.float32)
    for i, part in enumerate((high_part, mid_part, rest - mid_part)):
        part = part.reshape(SOURCES, span, LANES)
        packed = jnp.where((lane == row + i * ROWS)[None], part, packed)
    for rank in range(CAPACITY):
        mine = slice(rank * ROWS, (rank + 1) * ROWS)
        acc[:, rank, :ROWS, :] = out[:, mine, :]
        acc[:, rank, ROWS : ROWS + 1, :] = jnp.sum(packed[:, mine, :], axis=1, keepdims=True)
    ret_ref[...] = acc[...].astype(jnp.bfloat16)


def prefix_attention(recv, kv):
    sources = recv.shape[0]
    length = kv.shape[1]
    out_block = (SOURCES, CAPACITY, PAD_ROWS, LANES)
    return pl.pallas_call(
        prefix_kernel,
        grid=(sources // SOURCES,),
        out_shape=jax.ShapeDtypeStruct((sources,) + out_block[1:], jnp.bfloat16),
        in_specs=[
            pl.BlockSpec((SOURCES, CAPACITY * ROWS, LANES), lambda i: (i, 0, 0)),
            pl.BlockSpec((LANES, length), lambda i: (0, 0)),
        ],
        out_specs=pl.BlockSpec(out_block, lambda i: (i, 0, 0, 0)),
        scratch_shapes=[
            pltpu.VMEM((LANES, length), jnp.bfloat16),
            pltpu.VMEM(out_block, jnp.float32),
        ],
        compiler_params=pltpu.CompilerParams(vmem_limit_bytes=VMEM_LIMIT),
        cost_estimate=pl.CostEstimate(
            flops=8_000_000_000, bytes_accessed=4_000_000, transcendentals=0
        ),
        name="prefix",
    )(recv, kv)


def merge_kernel(code_ref, ret_ref, suffix_ref, suffix_lse_ref, w_ref, out_ref, picked, merged, left):
    requests = code_ref.shape[0]

    @pl.when(pl.program_id(0) == 0)
    def _():
        for r in range(requests):
            code = code_ref[r]
            picked[r] = ret_ref[code].astype(jnp.float32)
        lane = lane_iota(PAD_ROWS) % HALF
        row = lax.broadcasted_iota(jnp.int32, (PAD_ROWS, LANES), 0)
        own = jnp.logical_or(lane == row, jnp.logical_or(lane == row + ROWS, lane == row + 2 * ROWS))
        own = jnp.logical_and(own, row < ROWS)
        copies = jnp.where(own[None], picked[:, ROWS : ROWS + 1, :], 0.0).astype(jnp.bfloat16)
        same_half = lax.broadcasted_iota(jnp.int32, (LANES, LANES), 0) // HALF
        same_half = same_half == lane_iota(LANES) // HALF
        prefix_lse = jnp.dot(
            copies.reshape(requests * PAD_ROWS, LANES),
            same_half.astype(jnp.bfloat16),
            preferred_element_type=jnp.float32,
        )
        gap = prefix_lse - suffix_lse_ref[...]
        small = jnp.exp(-jnp.abs(gap))
        large_weight = 1.0 / (1.0 + small)
        small_weight = small * large_weight
        prefix_first = gap >= 0.0
        merged[...] = picked[...].reshape(requests * PAD_ROWS, LANES) * jnp.where(
            prefix_first, large_weight, small_weight
        ) + suffix_ref[...] * jnp.where(prefix_first, small_weight, large_weight)
        pairs = ROWS // STEPS
        for step in range(STEPS):
            for pair in range(pairs):
                left[step * requests : (step + 1) * requests, pair * LANES : (pair + 1) * LANES] = merged[
                    pl.ds(step * pairs + pair, requests, stride=PAD_ROWS), :
                ].astype(jnp.bfloat16)

    for core in range(CORES):
        out_ref[core, 0] = nt_dot(left[...], w_ref[core]).astype(jnp.bfloat16)


def merge_project(codes, ret, suffix_out, suffix_lse, weights, parts):
    requests = codes.shape[0]
    width = weights.shape[0] // parts
    depth = weights.shape[1]
    whole = lambda array: pl.BlockSpec(array.shape, lambda t: (0,) * array.ndim)
    return pl.pallas_call(
        merge_kernel,
        grid=(parts // CORES,),
        out_shape=jax.ShapeDtypeStruct((CORES, parts // CORES, STEPS * requests, width), jnp.bfloat16),
        in_specs=[
            pl.BlockSpec(memory_space=pltpu.SMEM),
            whole(ret),
            whole(suffix_out),
            whole(suffix_lse),
            pl.BlockSpec((CORES, width, depth), lambda t: (t, 0, 0)),
        ],
        out_specs=pl.BlockSpec((CORES, 1, STEPS * requests, width), lambda t: (0, t, 0, 0)),
        scratch_shapes=[
            pltpu.VMEM((requests, PAD_ROWS, LANES), jnp.float32),
            pltpu.VMEM((requests * PAD_ROWS, LANES), jnp.float32),
            pltpu.VMEM((STEPS * requests, depth), jnp.bfloat16),
        ],
        compiler_params=pltpu.CompilerParams(vmem_limit_bytes=VMEM_LIMIT),
        name="merge",
    )(codes, ret, suffix_out, suffix_lse, weights.reshape(parts, width, depth))


def shards(queries, prefix_cache, suffix_cache, suffix_lengths, request_prefix, prefix_owner, out_proj):
    tensor_size = lax.axis_size("tensor")
    me = lax.axis_index("prefix").astype(jnp.int32).reshape(1)
    q3 = queries.transpose(1, 0, 2)
    send, codes = route(me, request_prefix.reshape(-1), prefix_owner, q3)
    recv = lax.all_to_all(send, "prefix", split_axis=0, concat_axis=0, tiled=True)
    suffix_rows = suffix_cache[:, 0].transpose(0, 2, 1)
    suffix_out, suffix_lse = suffix_attention(suffix_lengths, q3, suffix_rows)
    recv, suffix_out, suffix_lse = lax.optimization_barrier((recv, suffix_out, suffix_lse))
    ret = prefix_attention(recv, prefix_cache[0, 0])
    ret = ret.reshape(ret.shape[0], CAPACITY * PAD_ROWS, LANES)
    homed = lax.all_to_all(ret, "prefix", split_axis=0, concat_axis=0, tiled=True)
    homed = homed.reshape(-1, PAD_ROWS, LANES)
    parts = merge_project(codes, homed, suffix_out, suffix_lse, out_proj.T, tensor_size)
    y_size = tensor_size // CORES
    core_groups = [[y * CORES + c for c in range(CORES)] for y in range(y_size)]
    y_groups = [[y * CORES + c for y in range(y_size)] for c in range(CORES)]
    for groups in (core_groups, y_groups):
        parts = lax.all_to_all(
            parts, "tensor", split_axis=0, concat_axis=0, axis_index_groups=groups, tiled=True
        )
        parts = jnp.sum(parts.astype(jnp.float32), axis=0).astype(jnp.bfloat16)
    return parts.reshape(STEPS, queries.shape[0], -1).transpose(1, 0, 2)


def solution(mesh):
    return jax.shard_map(
        shards,
        mesh=mesh,
        in_specs=(
            P("prefix", None, "tensor"),
            P("prefix", "tensor", None, None),
            P("prefix", "tensor", None, None),
            P("prefix"),
            P(),
            P(),
            P("tensor", None),
        ),
        out_specs=P("prefix", None, "tensor"),
        check_vma=False,
    )
```

```python
import functools

import jax
import jax.numpy as jnp
from jax import lax
from jax.experimental import pallas as pl
from jax.experimental.pallas import tpu as pltpu
from jax.sharding import PartitionSpec as P

LANES = 128
HALF = 64
X_SIZE = 4
CORES = 2
CAPACITY = 2
GROUPS = X_SIZE * CAPACITY
STEPS = 3
ROWS = 12
PAD_ROWS = 16
SCALE = 0.125
VMEM_LIMIT = 56 * 1024 * 1024


def lane_iota(rows):
    return lax.broadcasted_iota(jnp.int32, (rows, LANES), 1)


def split_heads(rows):
    low = lane_iota(rows.shape[0]) < HALF
    even = jnp.where(low, rows, 0.0)
    odd = jnp.where(low, pltpu.roll(rows, HALF, 1), 0.0)
    return even, odd


def join_heads(even, odd):
    low = lane_iota(even.shape[0]) < HALF
    return jnp.where(low, pltpu.roll(even, HALF, 1), odd)


def nt_dot(left, right):
    return lax.dot_general(
        left, right, (((1,), (1,)), ((), ())), preferred_element_type=jnp.float32
    )


def spread_queries(q_ref, qs):
    requests = q_ref.shape[1]
    for i in range(PAD_ROWS):
        if i < ROWS:
            step, pair = divmod(i, ROWS // STEPS)
            value = q_ref[step, :, pair * LANES : (pair + 1) * LANES].astype(jnp.float32)
        else:
            value = jnp.zeros((requests, LANES), jnp.float32)
        qs[pl.ds(i, requests, stride=PAD_ROWS), :] = value


def route_kernel(me_ref, prefix_ref, owner_ref, q_ref, send_ref, code_ref, taken, source, qs, acc):
    requests = q_ref.shape[1]
    z_size = send_ref.shape[0]
    me = me_ref[0]
    x_own = me & (X_SIZE - 1)
    for i in range(owner_ref.shape[0]):
        taken[i] = 0
    for i in range(z_size * GROUPS):
        source[i] = 0

    def place(r, _):
        name = prefix_ref[me * requests + r]
        owner = owner_ref[name]
        rank = taken[name]
        taken[name] = rank + 1
        offset = (owner - x_own) & (X_SIZE - 1)
        code = (owner >> 2) * GROUPS + (offset ^ (offset >> 1)) * CAPACITY + rank
        code_ref[r] = code
        source[code] = r
        return 0

    lax.fori_loop(0, requests, place, 0, unroll=8)
    spread_queries(q_ref, qs)

    def fill(z, _):
        for slot in range(GROUPS):
            r = source[z * GROUPS + slot]
            block = qs[pl.ds(pl.multiple_of(r * PAD_ROWS, PAD_ROWS), PAD_ROWS), :]
            acc[z, slot * ROWS : (slot + 1) * ROWS, :] = block[:ROWS]
        return 0

    lax.fori_loop(0, z_size, fill, 0, unroll=4)
    send_ref[...] = acc[...].astype(jnp.bfloat16)


def route(me, prefixes, owner, q3, z_size):
    requests = q3.shape[1]
    smem = pl.BlockSpec(memory_space=pltpu.SMEM)
    vmem = pl.BlockSpec(memory_space=pltpu.VMEM)
    shape = (z_size, GROUPS * ROWS, LANES)
    return pl.pallas_call(
        route_kernel,
        out_shape=(
            jax.ShapeDtypeStruct(shape, jnp.bfloat16),
            jax.ShapeDtypeStruct((requests,), jnp.int32),
        ),
        in_specs=[smem, smem, smem, vmem],
        out_specs=(vmem, smem),
        scratch_shapes=[
            pltpu.SMEM((owner.shape[0],), jnp.int32),
            pltpu.SMEM((z_size * GROUPS,), jnp.int32),
            pltpu.VMEM((requests * PAD_ROWS, LANES), jnp.float32),
            pltpu.VMEM(shape, jnp.float32),
        ],
        compiler_params=pltpu.CompilerParams(vmem_limit_bytes=VMEM_LIMIT),
        name="route",
    )(me, prefixes, owner, q3)


SUFFIX_BLOCK = 4


def suffix_kernel(length_ref, q_ref, kv_ref, out_ref, lse_ref, qs):
    spread_queries(q_ref, qs)
    requests, positions, _ = kv_ref.shape
    rows = SUFFIX_BLOCK * PAD_ROWS
    shape = (2 * rows, SUFFIX_BLOCK * positions)
    row = lax.broadcasted_iota(jnp.int32, shape, 0) % rows
    request = row // PAD_ROWS
    step = row % PAD_ROWS // (ROWS // STEPS)
    place = lax.broadcasted_iota(jnp.int32, shape, 1) - request * positions
    past = jnp.where(place >= 0, place - step, 2 * positions)
    request_rows = lax.broadcasted_iota(jnp.int32, (2 * rows, 1), 0) % rows // PAD_ROWS
    low = lane_iota(rows) < HALF

    def some(i, _):
        here = pl.ds(pl.multiple_of(i * rows, rows), rows)
        even, odd = split_heads(qs[here, :] * SCALE)
        query = jnp.concatenate([even, odd], axis=0).astype(jnp.bfloat16)
        cache = kv_ref[pl.ds(i * SUFFIX_BLOCK, SUFFIX_BLOCK)].reshape(-1, LANES)
        limit = jnp.zeros((2 * rows, 1), jnp.int32)
        for r in range(SUFFIX_BLOCK):
            limit = jnp.where(request_rows == r, length_ref[i * SUFFIX_BLOCK + r] - (STEPS - 1), limit)
        scores = jnp.where(past < limit, nt_dot(query, cache), -jnp.inf)
        highest = jnp.max(scores, axis=1, keepdims=True)
        weight = jnp.exp(scores - highest)
        total = jnp.sum(weight, axis=1, keepdims=True)
        mixed = jnp.dot(weight.astype(jnp.bfloat16), cache, preferred_element_type=jnp.float32)
        mixed = mixed / total
        lse = highest + jnp.log(total)
        out_ref[here, :] = join_heads(mixed[:rows], mixed[rows:])
        lse_ref[here, :] = jnp.where(low, lse[:rows], lse[rows:])
        return 0

    lax.fori_loop(0, requests // SUFFIX_BLOCK, some, 0, unroll=2)


def suffix_attention(lengths, q3, kv):
    requests = kv.shape[0]
    vmem = pl.BlockSpec(memory_space=pltpu.VMEM)
    shape = jax.ShapeDtypeStruct((requests * PAD_ROWS, LANES), jnp.float32)
    return pl.pallas_call(
        suffix_kernel,
        out_shape=(shape, shape),
        in_specs=[pl.BlockSpec(memory_space=pltpu.SMEM), vmem, vmem],
        out_specs=(vmem, vmem),
        scratch_shapes=[pltpu.VMEM((requests * PAD_ROWS, LANES), jnp.float32)],
        compiler_params=pltpu.CompilerParams(vmem_limit_bytes=VMEM_LIMIT),
        cost_estimate=pl.CostEstimate(
            flops=8_000_000_000, bytes_accessed=8_000_000, transcendentals=0
        ),
        name="suffix",
    )(lengths, q3, kv)


CHUNKS = 2
OFFSETS = (0, 1, 3, 2)


def prefix_kernel(first, count, *refs):
    recv_ref, sources = refs[0], refs[1 : 1 + count]
    before = refs[1 + count : len(refs) - 6]
    ret_ref, cache, values, queries, acc, sems = refs[-6:]
    index = pl.program_id(0)
    group = index + first
    z_size = recv_ref.shape[0]
    span = CAPACITY * ROWS
    rows = z_size * span
    copies = [pltpu.make_async_copy(sources[i], cache.at[i], sems.at[i]) for i in range(count)]

    @pl.when(index == 0)
    def _():
        for copy in copies:
            copy.start()
        queries[...] = recv_ref[...].astype(jnp.float32) * SCALE
        values[HALF:, :] = jnp.ones_like(values[HALF:, :])
        if before:
            acc[...] = before[0][...].astype(jnp.float32)

    for i in range(count):
        pl.when(index == i)(copies[i].wait)
    values[:HALF, :] = cache[index, HALF:]
    place = pl.ds(pl.multiple_of(group * span, 8), span)
    query = jnp.concatenate(split_heads(queries[:, place, :].reshape(rows, LANES)), axis=0)
    query = query.astype(jnp.bfloat16)
    size = 2 * rows // CHUNKS
    scores, weights, mixes = [None] * CHUNKS, [None] * CHUNKS, []
    for stage in range(CHUNKS + 2):
        if stage < CHUNKS:
            here = query[stage * size : (stage + 1) * size]
            scores[stage] = jnp.dot(here, cache[index], preferred_element_type=jnp.float32)
        if stage >= 2:
            weight, highest = weights[stage - 2]
            mixed = nt_dot(weight, values[...])
            low = lane_iota(size) < HALF
            total = jnp.where(low, pltpu.roll(mixed, HALF, 1), mixed)
            mixes.append((mixed / total, highest + jnp.log(total)))
        if 1 <= stage <= CHUNKS:
            highest = jnp.max(scores[stage - 1], axis=1, keepdims=True)
            weight = jnp.exp(scores[stage - 1] - highest).astype(jnp.bfloat16)
            weights[stage - 1] = (weight, highest)
    half = CHUNKS // 2
    low = lane_iota(size) < HALF
    lse = []
    for i in range(half):
        out = jnp.where(low, mixes[i][0], pltpu.roll(mixes[i + half][0], HALF, 1))
        sources = slice(i * z_size // half, (i + 1) * z_size // half)
        acc[sources, place, :] = out.reshape(z_size // half, span, LANES)
        lse.append(jnp.where(low, mixes[i][1], mixes[i + half][1]))
    lse = jnp.concatenate(lse, axis=0)
    lane = lax.broadcasted_iota(jnp.int32, (span, LANES), 1) & (HALF - 1)
    row = lax.broadcasted_iota(jnp.int32, (span, LANES), 0)
    row = jnp.where(row < ROWS, row, row - ROWS)
    high_part = lse.astype(jnp.bfloat16).astype(jnp.float32)
    rest = lse - high_part
    mid_part = rest.astype(jnp.bfloat16).astype(jnp.float32)
    packed = jnp.zeros((z_size, span, LANES), jnp.float32)
    for i, part in enumerate((high_part, mid_part, rest - mid_part)):
        part = part.reshape(z_size, span, LANES)
        packed = jnp.where((lane == row + i * ROWS)[None], part, packed)
    packed = packed.reshape(rows, LANES).astype(jnp.bfloat16)
    shape = (z_size * GROUPS, rows)
    slot = lax.broadcasted_iota(jnp.int32, shape, 0)
    inside = (slot & (GROUPS - 1)) // CAPACITY == group
    slot = slot // GROUPS * CAPACITY + (slot & (CAPACITY - 1))
    first = lax.broadcasted_iota(jnp.int32, shape, 1) - slot * ROWS
    pick = jnp.logical_and(inside, jnp.logical_and(first >= 0, first < ROWS))
    lse_rows = jnp.dot(pick.astype(jnp.bfloat16), packed, preferred_element_type=jnp.float32)
    lse_rows = lse_rows.reshape(z_size, GROUPS, LANES)
    own = lax.broadcasted_iota(jnp.int32, (GROUPS, LANES), 0) // CAPACITY == group
    acc[:, GROUPS * ROWS :, :] = jnp.where(own[None], lse_rows, acc[:, GROUPS * ROWS :, :])

    @pl.when(index == count - 1)
    def _():
        ret_ref[...] = acc[...].astype(jnp.bfloat16)


def prefix_attention(recv, caches, first, before=()):
    z_size = recv.shape[0]
    count = len(caches)
    length = caches[0].shape[1]
    out_shape = (z_size, GROUPS * ROWS + GROUPS, LANES)
    vmem = pl.BlockSpec(memory_space=pltpu.VMEM)
    return pl.pallas_call(
        functools.partial(prefix_kernel, first, count),
        grid=(count,),
        out_shape=jax.ShapeDtypeStruct(out_shape, jnp.bfloat16),
        in_specs=[vmem] + [pl.BlockSpec(memory_space=pl.ANY)] * count + [vmem] * len(before),
        out_specs=vmem,
        scratch_shapes=[
            pltpu.VMEM((count, LANES, length), jnp.bfloat16),
            pltpu.VMEM((LANES, length), jnp.bfloat16),
            pltpu.VMEM(recv.shape, jnp.float32),
            pltpu.VMEM(out_shape, jnp.float32),
            pltpu.SemaphoreType.DMA((count,)),
        ],
        compiler_params=pltpu.CompilerParams(vmem_limit_bytes=VMEM_LIMIT),
        cost_estimate=pl.CostEstimate(
            flops=2_500_000_000 * count, bytes_accessed=1_000_000 * count, transcendentals=0
        ),
        name="prefix",
    )(recv, *caches, *before)


def merge_kernel(code_ref, ret_ref, suffix_ref, suffix_lse_ref, w_ref, out_ref, wide, picked, packed, merged, left):
    requests = code_ref.shape[0]

    @pl.when(pl.program_id(0) == 0)
    def _():
        wide[...] = ret_ref[...].astype(jnp.float32)
        pair_rows = CAPACITY * ROWS
        for r in range(requests):
            code = code_ref[r]
            z, slot = code // GROUPS, code % GROUPS
            start = pl.multiple_of(slot // CAPACITY * pair_rows, 8)
            pair = wide[z, pl.ds(start, pair_rows), :]
            second = jnp.concatenate([pair[ROWS:], pair[: PAD_ROWS - ROWS]], axis=0)
            picked[r] = jnp.where(slot % CAPACITY == 0, pair[:PAD_ROWS], second)
            packed[r : r + 1, :] = wide[z, pl.ds(GROUPS * ROWS + slot, 1), :]
        lane = lane_iota(PAD_ROWS) % HALF
        row = lax.broadcasted_iota(jnp.int32, (PAD_ROWS, LANES), 0)
        own = jnp.logical_or(lane == row, jnp.logical_or(lane == row + ROWS, lane == row + 2 * ROWS))
        own = jnp.logical_and(own, row < ROWS)
        copies = jnp.where(own[None], packed[...][:, None, :], 0.0).astype(jnp.bfloat16)
        same_half = lax.broadcasted_iota(jnp.int32, (LANES, LANES), 0) // HALF
        same_half = same_half == lane_iota(LANES) // HALF
        prefix_lse = jnp.dot(
            copies.reshape(requests * PAD_ROWS, LANES),
            same_half.astype(jnp.bfloat16),
            preferred_element_type=jnp.float32,
        )
        gap = prefix_lse - suffix_lse_ref[...]
        small = jnp.exp(-jnp.abs(gap))
        large_weight = 1.0 / (1.0 + small)
        small_weight = small * large_weight
        prefix_first = gap >= 0.0
        merged[...] = picked[...].reshape(requests * PAD_ROWS, LANES) * jnp.where(
            prefix_first, large_weight, small_weight
        ) + suffix_ref[...] * jnp.where(prefix_first, small_weight, large_weight)
        pairs = ROWS // STEPS
        for step in range(STEPS):
            for pair in range(pairs):
                left[step * requests : (step + 1) * requests, pair * LANES : (pair + 1) * LANES] = merged[
                    pl.ds(step * pairs + pair, requests, stride=PAD_ROWS), :
                ].astype(jnp.bfloat16)

    for core in range(CORES):
        out_ref[core, 0] = nt_dot(left[...], w_ref[core]).astype(jnp.bfloat16)


def merge_project(codes, ret, suffix_out, suffix_lse, weights, parts):
    requests = codes.shape[0]
    width = weights.shape[0] // parts
    depth = weights.shape[1]
    whole = lambda array: pl.BlockSpec(array.shape, lambda t: (0,) * array.ndim)
    return pl.pallas_call(
        merge_kernel,
        grid=(parts // CORES,),
        out_shape=jax.ShapeDtypeStruct((CORES, parts // CORES, STEPS * requests, width), jnp.bfloat16),
        in_specs=[
            pl.BlockSpec(memory_space=pltpu.SMEM),
            whole(ret),
            whole(suffix_out),
            whole(suffix_lse),
            pl.BlockSpec((CORES, width, depth), lambda t: (t, 0, 0)),
        ],
        out_specs=pl.BlockSpec((CORES, 1, STEPS * requests, width), lambda t: (0, t, 0, 0)),
        scratch_shapes=[
            pltpu.VMEM(ret.shape, jnp.float32),
            pltpu.VMEM((requests, PAD_ROWS, LANES), jnp.float32),
            pltpu.VMEM((requests, LANES), jnp.float32),
            pltpu.VMEM((requests * PAD_ROWS, LANES), jnp.float32),
            pltpu.VMEM((STEPS * requests, depth), jnp.bfloat16),
        ],
        compiler_params=pltpu.CompilerParams(vmem_limit_bytes=VMEM_LIMIT),
        name="merge",
    )(codes, ret, suffix_out, suffix_lse, weights.reshape(parts, width, depth))


def shards(queries, prefix_cache, suffix_cache, suffix_lengths, request_prefix, prefix_owner, out_proj):
    prefix_size = lax.axis_size("prefix")
    tensor_size = lax.axis_size("tensor")
    z_size = prefix_size // X_SIZE
    z_groups = [[z * X_SIZE + x for z in range(z_size)] for x in range(X_SIZE)]
    me = lax.axis_index("prefix").astype(jnp.int32).reshape(1)
    kv = prefix_cache[0, 0]
    q3 = queries.transpose(1, 0, 2)
    send, codes = route(me, request_prefix.reshape(-1), prefix_owner, q3, z_size)
    kv_out, send = lax.optimization_barrier((kv, send))
    caches = [kv]
    for offset in OFFSETS[1:]:
        pairs = [
            (z * X_SIZE + (x + offset) % X_SIZE, z * X_SIZE + x)
            for z in range(z_size)
            for x in range(X_SIZE)
        ]
        caches.append(lax.ppermute(kv_out, "prefix", pairs))
    recv = lax.all_to_all(
        send, "prefix", split_axis=0, concat_axis=0, axis_index_groups=z_groups, tiled=True
    )
    suffix_rows = suffix_cache[:, 0].transpose(0, 2, 1)
    suffix_out, suffix_lse = suffix_attention(suffix_lengths, q3, suffix_rows)
    recv, suffix_out, suffix_lse = lax.optimization_barrier((recv, suffix_out, suffix_lse))
    ret = prefix_attention(recv, caches[:3], 0)
    ret = prefix_attention(recv, caches[3:], 3, (ret,))
    homed = lax.all_to_all(
        ret, "prefix", split_axis=0, concat_axis=0, axis_index_groups=z_groups, tiled=True
    )
    parts = merge_project(codes, homed, suffix_out, suffix_lse, out_proj.T, tensor_size)
    y_size = tensor_size // CORES
    core_groups = [[y * CORES + c for c in range(CORES)] for y in range(y_size)]
    y_groups = [[y * CORES + c for y in range(y_size)] for c in range(CORES)]
    for groups in (core_groups, y_groups):
        parts = lax.all_to_all(
            parts, "tensor", split_axis=0, concat_axis=0, axis_index_groups=groups, tiled=True
        )
        parts = jnp.sum(parts.astype(jnp.float32), axis=0).astype(jnp.bfloat16)
    return parts.reshape(STEPS, queries.shape[0], -1).transpose(1, 0, 2)


def solution(mesh):
    return jax.shard_map(
        shards,
        mesh=mesh,
        in_specs=(
            P("prefix", None, "tensor"),
            P("prefix", "tensor", None, None),
            P("prefix", "tensor", None, None),
            P("prefix"),
            P(),
            P(),
            P("tensor", None),
        ),
        out_specs=P("prefix", None, "tensor"),
        check_vma=False,
    )
```

```python
import functools

import jax
import jax.numpy as jnp
from jax import lax
from jax.experimental import pallas as pl
from jax.experimental.pallas import tpu as pltpu
from jax.sharding import PartitionSpec as P

LANES = 128
HALF = 64
X_SIZE = 4
CORES = 2
CAPACITY = 2
GROUPS = X_SIZE * CAPACITY
STEPS = 3
ROWS = 12
PAD_ROWS = 16
SCALE = 0.125
VMEM_LIMIT = 56 * 1024 * 1024


def lane_iota(rows):
    return lax.broadcasted_iota(jnp.int32, (rows, LANES), 1)


def split_heads(rows):
    low = lane_iota(rows.shape[0]) < HALF
    even = jnp.where(low, rows, 0.0)
    odd = jnp.where(low, pltpu.roll(rows, HALF, 1), 0.0)
    return even, odd


def join_heads(even, odd):
    low = lane_iota(even.shape[0]) < HALF
    return jnp.where(low, pltpu.roll(even, HALF, 1), odd)


def nt_dot(left, right):
    return lax.dot_general(
        left, right, (((1,), (1,)), ((), ())), preferred_element_type=jnp.float32
    )


def spread_queries(q_ref, qs):
    requests = q_ref.shape[1]
    for i in range(PAD_ROWS):
        if i < ROWS:
            step, pair = divmod(i, ROWS // STEPS)
            value = q_ref[step, :, pair * LANES : (pair + 1) * LANES].astype(jnp.float32)
        else:
            value = jnp.zeros((requests, LANES), jnp.float32)
        qs[pl.ds(i, requests, stride=PAD_ROWS), :] = value


def route_kernel(me_ref, prefix_ref, owner_ref, q_ref, send_ref, code_ref, taken, source, qs, acc):
    requests = q_ref.shape[1]
    z_size = send_ref.shape[0]
    me = me_ref[0]
    x_own = me & (X_SIZE - 1)
    for i in range(owner_ref.shape[0]):
        taken[i] = 0
    for i in range(z_size * GROUPS):
        source[i] = 0

    def place(r, _):
        name = prefix_ref[me * requests + r]
        owner = owner_ref[name]
        rank = taken[name]
        taken[name] = rank + 1
        offset = (owner - x_own) & (X_SIZE - 1)
        code = (owner >> 2) * GROUPS + (offset ^ (offset >> 1)) * CAPACITY + rank
        code_ref[r] = code
        source[code] = r
        return 0

    lax.fori_loop(0, requests, place, 0, unroll=8)
    spread_queries(q_ref, qs)

    def fill(z, _):
        for slot in range(GROUPS):
            r = source[z * GROUPS + slot]
            block = qs[pl.ds(pl.multiple_of(r * PAD_ROWS, PAD_ROWS), PAD_ROWS), :]
            acc[z, slot * ROWS : (slot + 1) * ROWS, :] = block[:ROWS]
        return 0

    lax.fori_loop(0, z_size, fill, 0, unroll=4)
    send_ref[...] = acc[...].astype(jnp.bfloat16)


def route(me, prefixes, owner, q3, z_size):
    requests = q3.shape[1]
    smem = pl.BlockSpec(memory_space=pltpu.SMEM)
    vmem = pl.BlockSpec(memory_space=pltpu.VMEM)
    shape = (z_size, GROUPS * ROWS, LANES)
    return pl.pallas_call(
        route_kernel,
        out_shape=(
            jax.ShapeDtypeStruct(shape, jnp.bfloat16),
            jax.ShapeDtypeStruct((requests,), jnp.int32),
        ),
        in_specs=[smem, smem, smem, vmem],
        out_specs=(vmem, smem),
        scratch_shapes=[
            pltpu.SMEM((owner.shape[0],), jnp.int32),
            pltpu.SMEM((z_size * GROUPS,), jnp.int32),
            pltpu.VMEM((requests * PAD_ROWS, LANES), jnp.float32),
            pltpu.VMEM(shape, jnp.float32),
        ],
        compiler_params=pltpu.CompilerParams(vmem_limit_bytes=VMEM_LIMIT),
        name="route",
    )(me, prefixes, owner, q3)


SUFFIX_BLOCK = 4


def suffix_kernel(length_ref, q_ref, kv_ref, out_ref, lse_ref, qs):
    spread_queries(q_ref, qs)
    requests, positions, _ = kv_ref.shape
    rows = SUFFIX_BLOCK * PAD_ROWS
    shape = (2 * rows, SUFFIX_BLOCK * positions)
    row = lax.broadcasted_iota(jnp.int32, shape, 0) % rows
    request = row // PAD_ROWS
    step = row % PAD_ROWS // (ROWS // STEPS)
    place = lax.broadcasted_iota(jnp.int32, shape, 1) - request * positions
    past = jnp.where(place >= 0, place - step, 2 * positions)
    request_rows = lax.broadcasted_iota(jnp.int32, (2 * rows, 1), 0) % rows // PAD_ROWS
    low = lane_iota(rows) < HALF

    def some(i, _):
        here = pl.ds(pl.multiple_of(i * rows, rows), rows)
        even, odd = split_heads(qs[here, :] * SCALE)
        query = jnp.concatenate([even, odd], axis=0).astype(jnp.bfloat16)
        cache = kv_ref[pl.ds(i * SUFFIX_BLOCK, SUFFIX_BLOCK)].reshape(-1, LANES)
        limit = jnp.zeros((2 * rows, 1), jnp.int32)
        for r in range(SUFFIX_BLOCK):
            limit = jnp.where(request_rows == r, length_ref[i * SUFFIX_BLOCK + r] - (STEPS - 1), limit)
        scores = jnp.where(past < limit, nt_dot(query, cache), -jnp.inf)
        highest = jnp.max(scores, axis=1, keepdims=True)
        weight = jnp.exp(scores - highest)
        total = jnp.sum(weight, axis=1, keepdims=True)
        mixed = jnp.dot(weight.astype(jnp.bfloat16), cache, preferred_element_type=jnp.float32)
        mixed = mixed / total
        lse = highest + jnp.log(total)
        out_ref[here, :] = join_heads(mixed[:rows], mixed[rows:])
        lse_ref[here, :] = jnp.where(low, lse[:rows], lse[rows:])
        return 0

    lax.fori_loop(0, requests // SUFFIX_BLOCK, some, 0, unroll=2)


def suffix_attention(lengths, q3, kv):
    requests = kv.shape[0]
    vmem = pl.BlockSpec(memory_space=pltpu.VMEM)
    shape = jax.ShapeDtypeStruct((requests * PAD_ROWS, LANES), jnp.float32)
    return pl.pallas_call(
        suffix_kernel,
        out_shape=(shape, shape),
        in_specs=[pl.BlockSpec(memory_space=pltpu.SMEM), vmem, vmem],
        out_specs=(vmem, vmem),
        scratch_shapes=[pltpu.VMEM((requests * PAD_ROWS, LANES), jnp.float32)],
        compiler_params=pltpu.CompilerParams(vmem_limit_bytes=VMEM_LIMIT),
        cost_estimate=pl.CostEstimate(
            flops=8_000_000_000, bytes_accessed=8_000_000, transcendentals=0
        ),
        name="suffix",
    )(lengths, q3, kv)


CHUNKS = 2


def prefix_kernel(count, start, recv_ref, *refs):
    sources = refs[: len(refs) - 8]
    ret_ref, cache, values, queries, acc, stage_out, sems, out_sem = refs[-8:]
    index = pl.program_id(0)
    z_size = recv_ref.shape[0]
    span = CAPACITY * ROWS
    rows = z_size * span
    per_group = 1 if count > 1 else 2
    copies = []
    for i in range(count):
        size = LANES // per_group
        copies.append(
            [
                pltpu.make_async_copy(
                    sources[i + p], cache.at[i, p * size : (p + 1) * size], sems.at[i + p]
                )
                for p in range(per_group)
            ]
        )

    @pl.when(index == 0)
    def _():
        for copy in sum(copies, []):
            copy.start()
        queries[...] = recv_ref[...].astype(jnp.float32) * SCALE
        values[HALF:, :] = jnp.ones_like(values[HALF:, :])
        acc[...] = jnp.zeros_like(acc)

    group = index + (X_SIZE - count if start else 0)
    for i in range(count):

        @pl.when(index == i)
        def _():
            for copy in copies[i]:
                copy.wait()

    values[:HALF, :] = cache[index, HALF:]
    place = pl.ds(pl.multiple_of(group * span, 8), span)
    own_place = pl.ds(pl.multiple_of(index * span, 8), span)
    query = jnp.concatenate(split_heads(queries[:, place, :].reshape(rows, LANES)), axis=0)
    query = query.astype(jnp.bfloat16)
    size = 2 * rows // CHUNKS
    scores, weights, mixes = [None] * CHUNKS, [None] * CHUNKS, []
    for stage in range(CHUNKS + 2):
        if stage < CHUNKS:
            here = query[stage * size : (stage + 1) * size]
            scores[stage] = jnp.dot(here, cache[index], preferred_element_type=jnp.float32)
        if stage >= 2:
            weight, highest = weights[stage - 2]
            mixed = nt_dot(weight, values[...])
            low = lane_iota(size) < HALF
            total = jnp.where(low, pltpu.roll(mixed, HALF, 1), mixed)
            mixes.append((mixed / total, highest + jnp.log(total)))
        if 1 <= stage <= CHUNKS:
            highest = jnp.max(scores[stage - 1], axis=1, keepdims=True)
            weight = jnp.exp(scores[stage - 1] - highest).astype(jnp.bfloat16)
            weights[stage - 1] = (weight, highest)
    half = CHUNKS // 2
    low = lane_iota(size) < HALF
    lse = []
    for i in range(half):
        out = jnp.where(low, mixes[i][0], pltpu.roll(mixes[i + half][0], HALF, 1))
        sources = slice(i * z_size // half, (i + 1) * z_size // half)
        acc[sources, own_place, :] = out.reshape(z_size // half, span, LANES)
        lse.append(jnp.where(low, mixes[i][1], mixes[i + half][1]))
    lse = jnp.concatenate(lse, axis=0)
    lane = lax.broadcasted_iota(jnp.int32, (span, LANES), 1) & (HALF - 1)
    row = lax.broadcasted_iota(jnp.int32, (span, LANES), 0)
    row = jnp.where(row < ROWS, row, row - ROWS)
    high_part = lse.astype(jnp.bfloat16).astype(jnp.float32)
    rest = lse - high_part
    mid_part = rest.astype(jnp.bfloat16).astype(jnp.float32)
    packed = jnp.zeros((z_size, span, LANES), jnp.float32)
    for i, part in enumerate((high_part, mid_part, rest - mid_part)):
        part = part.reshape(z_size, span, LANES)
        packed = jnp.where((lane == row + i * ROWS)[None], part, packed)
    packed = packed.reshape(rows, LANES).astype(jnp.bfloat16)
    shape = (z_size * GROUPS, rows)
    slot = lax.broadcasted_iota(jnp.int32, shape, 0)
    inside = (slot & (GROUPS - 1)) // CAPACITY == index
    slot = slot // GROUPS * CAPACITY + (slot & (CAPACITY - 1))
    first = lax.broadcasted_iota(jnp.int32, shape, 1) - slot * ROWS
    pick = jnp.logical_and(inside, jnp.logical_and(first >= 0, first < ROWS))
    lse_rows = jnp.dot(pick.astype(jnp.bfloat16), packed, preferred_element_type=jnp.float32)
    lse_rows = lse_rows.reshape(z_size, GROUPS, LANES)
    own = lax.broadcasted_iota(jnp.int32, (GROUPS, LANES), 0) // CAPACITY == index
    acc[:, count * span :, :] = jnp.where(own[None], lse_rows, acc[:, count * span :, :])

    @pl.when(index == count - 1)
    def _():
        stage_out[...] = acc[...].astype(jnp.bfloat16)
        copy = pltpu.make_async_copy(
            stage_out, ret_ref.at[:, start : start + stage_out.shape[1], :], out_sem
        )
        copy.start()
        copy.wait()


FIRST_GROUPS = 3
FIRST_ROWS = FIRST_GROUPS * CAPACITY * ROWS + GROUPS
ALL_ROWS = FIRST_ROWS + CAPACITY * ROWS + GROUPS


def prefix_attention(recv, caches, before=None):
    z_size = recv.shape[0]
    count = len(caches) if before is None else 1
    start = 0 if before is None else FIRST_ROWS
    length = caches[0].shape[1]
    rows = count * CAPACITY * ROWS + GROUPS
    vmem = pl.BlockSpec(memory_space=pltpu.VMEM)
    anywhere = pl.BlockSpec(memory_space=pl.ANY)
    kernel = functools.partial(prefix_kernel, count, start)
    operands = [recv, *caches]
    aliases = {}
    if before is not None:
        aliases = {len(operands): 0}
        operands.append(before)
        inner = kernel
        kernel = lambda *refs: inner(*refs[:3], *refs[4:])
    return pl.pallas_call(
        kernel,
        grid=(count,),
        out_shape=jax.ShapeDtypeStruct((z_size, ALL_ROWS, LANES), jnp.bfloat16),
        in_specs=[vmem] + [anywhere] * (len(operands) - 1),
        out_specs=anywhere,
        scratch_shapes=[
            pltpu.VMEM((count, LANES, length), jnp.bfloat16),
            pltpu.VMEM((LANES, length), jnp.bfloat16),
            pltpu.VMEM(recv.shape, jnp.float32),
            pltpu.VMEM((z_size, rows, LANES), jnp.float32),
            pltpu.VMEM((z_size, rows, LANES), jnp.bfloat16),
            pltpu.SemaphoreType.DMA((len(caches),)),
            pltpu.SemaphoreType.DMA,
        ],
        input_output_aliases=aliases,
        compiler_params=pltpu.CompilerParams(vmem_limit_bytes=VMEM_LIMIT),
        cost_estimate=pl.CostEstimate(
            flops=2_500_000_000 * count, bytes_accessed=1_000_000 * count, transcendentals=0
        ),
        name="prefix",
    )(*operands)


def merge_kernel(code_ref, ret_ref, suffix_ref, suffix_lse_ref, w_ref, out_ref, wide, picked, packed, merged, left):
    requests = code_ref.shape[0]

    @pl.when(pl.program_id(0) == 0)
    def _():
        wide[...] = ret_ref[...].astype(jnp.float32)
        pair_rows = CAPACITY * ROWS
        for r in range(requests):
            code = code_ref[r]
            z, slot = code // GROUPS, code % GROUPS
            group = slot // CAPACITY
            last = group == FIRST_GROUPS
            start = pl.multiple_of(jnp.where(last, FIRST_ROWS, group * pair_rows), 8)
            lse_row = slot + jnp.where(
                last, ALL_ROWS - GROUPS - FIRST_GROUPS * CAPACITY, FIRST_ROWS - GROUPS
            )
            pair = wide[z, pl.ds(start, pair_rows), :]
            second = jnp.concatenate([pair[ROWS:], pair[: PAD_ROWS - ROWS]], axis=0)
            picked[r] = jnp.where(slot % CAPACITY == 0, pair[:PAD_ROWS], second)
            packed[r : r + 1, :] = wide[z, pl.ds(lse_row, 1), :]
        lane = lane_iota(PAD_ROWS) % HALF
        row = lax.broadcasted_iota(jnp.int32, (PAD_ROWS, LANES), 0)
        own = jnp.logical_or(lane == row, jnp.logical_or(lane == row + ROWS, lane == row + 2 * ROWS))
        own = jnp.logical_and(own, row < ROWS)
        copies = jnp.where(own[None], packed[...][:, None, :], 0.0).astype(jnp.bfloat16)
        same_half = lax.broadcasted_iota(jnp.int32, (LANES, LANES), 0) // HALF
        same_half = same_half == lane_iota(LANES) // HALF
        prefix_lse = jnp.dot(
            copies.reshape(requests * PAD_ROWS, LANES),
            same_half.astype(jnp.bfloat16),
            preferred_element_type=jnp.float32,
        )
        gap = prefix_lse - suffix_lse_ref[...]
        small = jnp.exp(-jnp.abs(gap))
        large_weight = 1.0 / (1.0 + small)
        small_weight = small * large_weight
        prefix_first = gap >= 0.0
        merged[...] = picked[...].reshape(requests * PAD_ROWS, LANES) * jnp.where(
            prefix_first, large_weight, small_weight
        ) + suffix_ref[...] * jnp.where(prefix_first, small_weight, large_weight)
        pairs = ROWS // STEPS
        for step in range(STEPS):
            for pair in range(pairs):
                left[step * requests : (step + 1) * requests, pair * LANES : (pair + 1) * LANES] = merged[
                    pl.ds(step * pairs + pair, requests, stride=PAD_ROWS), :
                ].astype(jnp.bfloat16)

    for core in range(CORES):
        out_ref[core, 0] = nt_dot(left[...], w_ref[core]).astype(jnp.bfloat16)


def merge_project(codes, ret, suffix_out, suffix_lse, weights, parts):
    requests = codes.shape[0]
    width = weights.shape[0] // parts
    depth = weights.shape[1]
    whole = lambda array: pl.BlockSpec(array.shape, lambda t: (0,) * array.ndim)
    return pl.pallas_call(
        merge_kernel,
        grid=(parts // CORES,),
        out_shape=jax.ShapeDtypeStruct((CORES, parts // CORES, STEPS * requests, width), jnp.bfloat16),
        in_specs=[
            pl.BlockSpec(memory_space=pltpu.SMEM),
            whole(ret),
            whole(suffix_out),
            whole(suffix_lse),
            pl.BlockSpec((CORES, width, depth), lambda t: (t, 0, 0)),
        ],
        out_specs=pl.BlockSpec((CORES, 1, STEPS * requests, width), lambda t: (0, t, 0, 0)),
        scratch_shapes=[
            pltpu.VMEM(ret.shape, jnp.float32),
            pltpu.VMEM((requests, PAD_ROWS, LANES), jnp.float32),
            pltpu.VMEM((requests, LANES), jnp.float32),
            pltpu.VMEM((requests * PAD_ROWS, LANES), jnp.float32),
            pltpu.VMEM((STEPS * requests, depth), jnp.bfloat16),
        ],
        compiler_params=pltpu.CompilerParams(vmem_limit_bytes=VMEM_LIMIT),
        name="merge",
    )(codes, ret, suffix_out, suffix_lse, weights.reshape(parts, width, depth))


def shards(queries, prefix_cache, suffix_cache, suffix_lengths, request_prefix, prefix_owner, out_proj):
    prefix_size = lax.axis_size("prefix")
    tensor_size = lax.axis_size("tensor")
    z_size = prefix_size // X_SIZE
    z_groups = [[z * X_SIZE + x for z in range(z_size)] for x in range(X_SIZE)]
    me = lax.axis_index("prefix").astype(jnp.int32).reshape(1)
    kv = prefix_cache[0, 0]
    q3 = queries.transpose(1, 0, 2)
    send, codes = route(me, request_prefix.reshape(-1), prefix_owner, q3, z_size)
    kv_out, send = lax.optimization_barrier((kv, send))

    def from_offset(array, offset):
        pairs = [
            (z * X_SIZE + (x + offset) % X_SIZE, z * X_SIZE + x)
            for z in range(z_size)
            for x in range(X_SIZE)
        ]
        return lax.ppermute(array, "prefix", pairs)

    right = from_offset(kv_out, 1)
    left = from_offset(kv_out, -1)
    opposite = (from_offset(right[:HALF], 1), from_offset(left[HALF:], -1))
    recv = lax.all_to_all(
        send, "prefix", split_axis=0, concat_axis=0, axis_index_groups=z_groups, tiled=True
    )
    suffix_rows = suffix_cache[:, 0].transpose(0, 2, 1)
    suffix_out, suffix_lse = suffix_attention(suffix_lengths, q3, suffix_rows)
    recv, suffix_out, suffix_lse = lax.optimization_barrier((recv, suffix_out, suffix_lse))
    ret = prefix_attention(recv, (kv, right, left))
    ret = prefix_attention(recv, opposite, ret)
    homed = lax.all_to_all(
        ret, "prefix", split_axis=0, concat_axis=0, axis_index_groups=z_groups, tiled=True
    )
    parts = merge_project(codes, homed, suffix_out, suffix_lse, out_proj.T, tensor_size)
    y_size = tensor_size // CORES
    core_groups = [[y * CORES + c for c in range(CORES)] for y in range(y_size)]
    y_groups = [[y * CORES + c for y in range(y_size)] for c in range(CORES)]
    for groups in (core_groups, y_groups):
        parts = lax.all_to_all(
            parts, "tensor", split_axis=0, concat_axis=0, axis_index_groups=groups, tiled=True
        )
        parts = jnp.sum(parts.astype(jnp.float32), axis=0).astype(jnp.bfloat16)
    return parts.reshape(STEPS, queries.shape[0], -1).transpose(1, 0, 2)


def solution(mesh):
    return jax.shard_map(
        shards,
        mesh=mesh,
        in_specs=(
            P("prefix", None, "tensor"),
            P("prefix", "tensor", None, None),
            P("prefix", "tensor", None, None),
            P("prefix"),
            P(),
            P(),
            P("tensor", None),
        ),
        out_specs=P("prefix", None, "tensor"),
        check_vma=False,
    )
```

```python
import functools

import jax
import jax.numpy as jnp
from jax import lax
from jax.experimental import pallas as pl
from jax.experimental.pallas import tpu as pltpu
from jax.sharding import PartitionSpec as P

LANES = 128
HALF = 64
X_SIZE = 4
CORES = 2
CAPACITY = 2
GROUPS = X_SIZE * CAPACITY
STEPS = 3
ROWS = 12
PAD_ROWS = 16
SCALE = 0.125
VMEM_LIMIT = 56 * 1024 * 1024
SMALL_LIMIT = 32 * 1024 * 1024


def lane_iota(rows):
    return lax.broadcasted_iota(jnp.int32, (rows, LANES), 1)


def split_heads(rows):
    low = lane_iota(rows.shape[0]) < HALF
    even = jnp.where(low, rows, 0.0)
    odd = jnp.where(low, pltpu.roll(rows, HALF, 1), 0.0)
    return even, odd


def join_heads(even, odd):
    low = lane_iota(even.shape[0]) < HALF
    return jnp.where(low, pltpu.roll(even, HALF, 1), odd)


def nt_dot(left, right):
    return lax.dot_general(
        left, right, (((1,), (1,)), ((), ())), preferred_element_type=jnp.float32
    )


def spread_queries(q_ref, qs):
    requests = q_ref.shape[1]
    for i in range(PAD_ROWS):
        if i < ROWS:
            step, pair = divmod(i, ROWS // STEPS)
            value = q_ref[step, :, pair * LANES : (pair + 1) * LANES].astype(jnp.float32)
        else:
            value = jnp.zeros((requests, LANES), jnp.float32)
        qs[pl.ds(i, requests, stride=PAD_ROWS), :] = value


def route_kernel(me_ref, prefix_ref, owner_ref, q_ref, send_ref, code_ref, taken, source, qs, acc):
    requests = q_ref.shape[1]
    z_size = send_ref.shape[0]
    me = me_ref[0]
    x_own = me & (X_SIZE - 1)
    for i in range(owner_ref.shape[0]):
        taken[i] = 0
    for i in range(z_size * GROUPS):
        source[i] = 0

    def place(r, _):
        name = prefix_ref[me * requests + r]
        owner = owner_ref[name]
        rank = taken[name]
        taken[name] = rank + 1
        offset = (owner - x_own) & (X_SIZE - 1)
        code = (owner >> 2) * GROUPS + (offset ^ (offset >> 1)) * CAPACITY + rank
        code_ref[r] = code
        source[code] = r
        return 0

    lax.fori_loop(0, requests, place, 0, unroll=8)
    spread_queries(q_ref, qs)

    def fill(z, _):
        for slot in range(GROUPS):
            r = source[z * GROUPS + slot]
            block = qs[pl.ds(pl.multiple_of(r * PAD_ROWS, PAD_ROWS), PAD_ROWS), :]
            acc[z, slot * ROWS : (slot + 1) * ROWS, :] = block[:ROWS]
        return 0

    lax.fori_loop(0, z_size, fill, 0, unroll=4)
    send_ref[...] = acc[...].astype(jnp.bfloat16)


def route(me, prefixes, owner, q3, z_size):
    requests = q3.shape[1]
    smem = pl.BlockSpec(memory_space=pltpu.SMEM)
    vmem = pl.BlockSpec(memory_space=pltpu.VMEM)
    shape = (z_size, GROUPS * ROWS, LANES)
    return pl.pallas_call(
        route_kernel,
        out_shape=(
            jax.ShapeDtypeStruct(shape, jnp.bfloat16),
            jax.ShapeDtypeStruct((requests,), jnp.int32),
        ),
        in_specs=[smem, smem, smem, vmem],
        out_specs=(vmem, smem),
        scratch_shapes=[
            pltpu.SMEM((owner.shape[0],), jnp.int32),
            pltpu.SMEM((z_size * GROUPS,), jnp.int32),
            pltpu.VMEM((requests * PAD_ROWS, LANES), jnp.float32),
            pltpu.VMEM(shape, jnp.float32),
        ],
        compiler_params=pltpu.CompilerParams(vmem_limit_bytes=VMEM_LIMIT),
        name="route",
    )(me, prefixes, owner, q3)


SUFFIX_BLOCK = 4


def suffix_kernel(length_ref, q_ref, kv_ref, out_ref, lse_ref, qs):
    spread_queries(q_ref, qs)
    requests, positions, _ = kv_ref.shape
    rows = SUFFIX_BLOCK * PAD_ROWS
    shape = (2 * rows, SUFFIX_BLOCK * positions)
    row = lax.broadcasted_iota(jnp.int32, shape, 0) % rows
    request = row // PAD_ROWS
    step = row % PAD_ROWS // (ROWS // STEPS)
    place = lax.broadcasted_iota(jnp.int32, shape, 1) - request * positions
    past = jnp.where(place >= 0, place - step, 2 * positions)
    request_rows = lax.broadcasted_iota(jnp.int32, (2 * rows, 1), 0) % rows // PAD_ROWS
    low = lane_iota(rows) < HALF

    def some(i, _):
        here = pl.ds(pl.multiple_of(i * rows, rows), rows)
        even, odd = split_heads(qs[here, :] * SCALE)
        query = jnp.concatenate([even, odd], axis=0).astype(jnp.bfloat16)
        cache = kv_ref[pl.ds(i * SUFFIX_BLOCK, SUFFIX_BLOCK)].reshape(-1, LANES)
        limit = jnp.zeros((2 * rows, 1), jnp.int32)
        for r in range(SUFFIX_BLOCK):
            limit = jnp.where(request_rows == r, length_ref[i * SUFFIX_BLOCK + r] - (STEPS - 1), limit)
        scores = jnp.where(past < limit, nt_dot(query, cache), -jnp.inf)
        highest = jnp.max(scores, axis=1, keepdims=True)
        weight = jnp.exp(scores - highest)
        total = jnp.sum(weight, axis=1, keepdims=True)
        mixed = jnp.dot(weight.astype(jnp.bfloat16), cache, preferred_element_type=jnp.float32)
        mixed = mixed / total
        lse = highest + jnp.log(total)
        out_ref[here, :] = join_heads(mixed[:rows], mixed[rows:])
        lse_ref[here, :] = jnp.where(low, lse[:rows], lse[rows:])
        return 0

    lax.fori_loop(0, requests // SUFFIX_BLOCK, some, 0, unroll=2)


def suffix_attention(lengths, q3, kv):
    requests = kv.shape[0]
    vmem = pl.BlockSpec(memory_space=pltpu.VMEM)
    shape = jax.ShapeDtypeStruct((requests * PAD_ROWS, LANES), jnp.float32)
    return pl.pallas_call(
        suffix_kernel,
        out_shape=(shape, shape),
        in_specs=[pl.BlockSpec(memory_space=pltpu.SMEM), vmem, vmem],
        out_specs=(vmem, vmem),
        scratch_shapes=[pltpu.VMEM((requests * PAD_ROWS, LANES), jnp.float32)],
        compiler_params=pltpu.CompilerParams(vmem_limit_bytes=VMEM_LIMIT),
        cost_estimate=pl.CostEstimate(
            flops=8_000_000_000, bytes_accessed=8_000_000, transcendentals=0
        ),
        name="suffix",
    )(lengths, q3, kv)


CHUNKS = 2


def prefix_kernel(count, start, recv_ref, *refs):
    sources = refs[: len(refs) - 8]
    ret_ref, cache, values, queries, acc, stage_out, sems, out_sem = refs[-8:]
    index = pl.program_id(0)
    z_size = recv_ref.shape[0]
    span = CAPACITY * ROWS
    rows = z_size * span
    copies = [pltpu.make_async_copy(sources[i], cache.at[i], sems.at[i]) for i in range(count)]

    @pl.when(index == 0)
    def _():
        for copy in copies:
            copy.start()
        queries[...] = recv_ref[...].astype(jnp.float32) * SCALE
        values[HALF:, :] = jnp.ones_like(values[HALF:, :])
        acc[...] = jnp.zeros_like(acc)

    group = index + (X_SIZE - count if start else 0)
    for i in range(count):
        pl.when(index == i)(copies[i].wait)
    values[:HALF, :] = cache[index, HALF:]
    place = pl.ds(pl.multiple_of(group * span, 8), span)
    own_place = pl.ds(pl.multiple_of(index * span, 8), span)
    query = jnp.concatenate(split_heads(queries[:, place, :].reshape(rows, LANES)), axis=0)
    query = query.astype(jnp.bfloat16)
    size = 2 * rows // CHUNKS
    scores, weights, mixes = [None] * CHUNKS, [None] * CHUNKS, []
    for stage in range(CHUNKS + 2):
        if stage < CHUNKS:
            here = query[stage * size : (stage + 1) * size]
            scores[stage] = jnp.dot(here, cache[index], preferred_element_type=jnp.float32)
        if stage >= 2:
            weight, highest = weights[stage - 2]
            mixed = nt_dot(weight, values[...])
            low = lane_iota(size) < HALF
            total = jnp.where(low, pltpu.roll(mixed, HALF, 1), mixed)
            mixes.append((mixed / total, highest + jnp.log(total)))
        if 1 <= stage <= CHUNKS:
            highest = jnp.max(scores[stage - 1], axis=1, keepdims=True)
            weight = jnp.exp(scores[stage - 1] - highest).astype(jnp.bfloat16)
            weights[stage - 1] = (weight, highest)
    half = CHUNKS // 2
    low = lane_iota(size) < HALF
    lse = []
    for i in range(half):
        out = jnp.where(low, mixes[i][0], pltpu.roll(mixes[i + half][0], HALF, 1))
        sources = slice(i * z_size // half, (i + 1) * z_size // half)
        acc[sources, own_place, :] = out.reshape(z_size // half, span, LANES)
        lse.append(jnp.where(low, mixes[i][1], mixes[i + half][1]))
    lse = jnp.concatenate(lse, axis=0)
    lane = lax.broadcasted_iota(jnp.int32, (span, LANES), 1) & (HALF - 1)
    row = lax.broadcasted_iota(jnp.int32, (span, LANES), 0)
    row = jnp.where(row < ROWS, row, row - ROWS)
    high_part = lse.astype(jnp.bfloat16).astype(jnp.float32)
    rest = lse - high_part
    mid_part = rest.astype(jnp.bfloat16).astype(jnp.float32)
    packed = jnp.zeros((z_size, span, LANES), jnp.float32)
    for i, part in enumerate((high_part, mid_part, rest - mid_part)):
        part = part.reshape(z_size, span, LANES)
        packed = jnp.where((lane == row + i * ROWS)[None], part, packed)
    packed = packed.reshape(rows, LANES).astype(jnp.bfloat16)
    shape = (z_size * GROUPS, rows)
    slot = lax.broadcasted_iota(jnp.int32, shape, 0)
    inside = (slot & (GROUPS - 1)) // CAPACITY == index
    slot = slot // GROUPS * CAPACITY + (slot & (CAPACITY - 1))
    first = lax.broadcasted_iota(jnp.int32, shape, 1) - slot * ROWS
    pick = jnp.logical_and(inside, jnp.logical_and(first >= 0, first < ROWS))
    lse_rows = jnp.dot(pick.astype(jnp.bfloat16), packed, preferred_element_type=jnp.float32)
    lse_rows = lse_rows.reshape(z_size, GROUPS, LANES)
    own = lax.broadcasted_iota(jnp.int32, (GROUPS, LANES), 0) // CAPACITY == index
    acc[:, count * span :, :] = jnp.where(own[None], lse_rows, acc[:, count * span :, :])

    @pl.when(index == count - 1)
    def _():
        stage_out[...] = acc[...].astype(jnp.bfloat16)
        copy = pltpu.make_async_copy(
            stage_out, ret_ref.at[:, start : start + stage_out.shape[1], :], out_sem
        )
        copy.start()
        copy.wait()


FIRST_GROUPS = 3
FIRST_ROWS = FIRST_GROUPS * CAPACITY * ROWS + GROUPS
ALL_ROWS = FIRST_ROWS + CAPACITY * ROWS + GROUPS


def prefix_attention(recv, caches, before=None):
    z_size = recv.shape[0]
    count = len(caches)
    start = 0 if before is None else FIRST_ROWS
    length = caches[0].shape[1]
    rows = count * CAPACITY * ROWS + GROUPS
    vmem = pl.BlockSpec(memory_space=pltpu.VMEM)
    anywhere = pl.BlockSpec(memory_space=pl.ANY)
    kernel = functools.partial(prefix_kernel, count, start)
    operands = [recv, *caches]
    aliases = {}
    if before is not None:
        aliases = {len(operands): 0}
        operands.append(before)
        inner = kernel
        kernel = lambda *refs: inner(*refs[:2], *refs[3:])
    return pl.pallas_call(
        kernel,
        grid=(count,),
        out_shape=jax.ShapeDtypeStruct((z_size, ALL_ROWS, LANES), jnp.bfloat16),
        in_specs=[vmem] + [anywhere] * (len(operands) - 1),
        out_specs=anywhere,
        scratch_shapes=[
            pltpu.VMEM((count, LANES, length), jnp.bfloat16),
            pltpu.VMEM((LANES, length), jnp.bfloat16),
            pltpu.VMEM(recv.shape, jnp.float32),
            pltpu.VMEM((z_size, rows, LANES), jnp.float32),
            pltpu.VMEM((z_size, rows, LANES), jnp.bfloat16),
            pltpu.SemaphoreType.DMA((count,)),
            pltpu.SemaphoreType.DMA,
        ],
        input_output_aliases=aliases,
        compiler_params=pltpu.CompilerParams(vmem_limit_bytes=SMALL_LIMIT),
        cost_estimate=pl.CostEstimate(
            flops=2_500_000_000 * count, bytes_accessed=1_000_000 * count, transcendentals=0
        ),
        name="prefix",
    )(*operands)


def merge_kernel(core_ref, code_ref, ret_ref, suffix_ref, suffix_lse_ref, w_ref, out_ref, left, wide, picked, packed, merged):
    requests = code_ref.shape[0]

    @pl.when(pl.program_id(0) == 0)
    def _():
        wide[...] = ret_ref[...].astype(jnp.float32)
        pair_rows = CAPACITY * ROWS
        for r in range(requests):
            code = code_ref[r]
            z, slot = code // GROUPS, code % GROUPS
            group = slot // CAPACITY
            last = group == FIRST_GROUPS
            start = pl.multiple_of(jnp.where(last, FIRST_ROWS, group * pair_rows), 8)
            lse_row = slot + jnp.where(
                last, ALL_ROWS - GROUPS - FIRST_GROUPS * CAPACITY, FIRST_ROWS - GROUPS
            )
            pair = wide[z, pl.ds(start, pair_rows), :]
            second = jnp.concatenate([pair[ROWS:], pair[: PAD_ROWS - ROWS]], axis=0)
            picked[r] = jnp.where(slot % CAPACITY == 0, pair[:PAD_ROWS], second)
            packed[r : r + 1, :] = wide[z, pl.ds(lse_row, 1), :]
        lane = lane_iota(PAD_ROWS) % HALF
        row = lax.broadcasted_iota(jnp.int32, (PAD_ROWS, LANES), 0)
        own = jnp.logical_or(lane == row, jnp.logical_or(lane == row + ROWS, lane == row + 2 * ROWS))
        own = jnp.logical_and(own, row < ROWS)
        copies = jnp.where(own[None], packed[...][:, None, :], 0.0).astype(jnp.bfloat16)
        same_half = lax.broadcasted_iota(jnp.int32, (LANES, LANES), 0) // HALF
        same_half = same_half == lane_iota(LANES) // HALF
        prefix_lse = jnp.dot(
            copies.reshape(requests * PAD_ROWS, LANES),
            same_half.astype(jnp.bfloat16),
            preferred_element_type=jnp.float32,
        )
        gap = prefix_lse - suffix_lse_ref[...]
        small = jnp.exp(-jnp.abs(gap))
        large_weight = 1.0 / (1.0 + small)
        small_weight = small * large_weight
        prefix_first = gap >= 0.0
        merged[...] = picked[...].reshape(requests * PAD_ROWS, LANES) * jnp.where(
            prefix_first, large_weight, small_weight
        ) + suffix_ref[...] * jnp.where(prefix_first, small_weight, large_weight)
        pairs = ROWS // STEPS
        for step in range(STEPS):
            for pair in range(pairs):
                left[step * requests : (step + 1) * requests, pair * LANES : (pair + 1) * LANES] = merged[
                    pl.ds(step * pairs + pair, requests, stride=PAD_ROWS), :
                ].astype(jnp.bfloat16)

    out_ref[0] = nt_dot(left[...], w_ref[0]).astype(jnp.bfloat16)


def project_kernel(core_ref, left_ref, w_ref, out_ref):
    out_ref[0] = nt_dot(left_ref[...], w_ref[0]).astype(jnp.bfloat16)


def merge_project(core, codes, ret, suffix_out, suffix_lse, weights, parts):
    requests = codes.shape[0]
    width = weights.shape[0] // parts
    depth = weights.shape[1]
    rows = STEPS * requests
    weights = weights.reshape(parts, width, depth)
    whole = lambda shape: pl.BlockSpec(shape, lambda t, core: (0,) * len(shape))
    out_spec = pl.BlockSpec((1, rows, width), lambda t, core: (t, 0, 0))
    out_shape = jax.ShapeDtypeStruct((parts // CORES, rows, width), jnp.bfloat16)
    other, left = pl.pallas_call(
        merge_kernel,
        out_shape=(out_shape, jax.ShapeDtypeStruct((rows, depth), jnp.bfloat16)),
        grid_spec=pltpu.PrefetchScalarGridSpec(
            num_scalar_prefetch=1,
            grid=(parts // CORES,),
            in_specs=[
                pl.BlockSpec(memory_space=pltpu.SMEM),
                whole(ret.shape),
                whole(suffix_out.shape),
                whole(suffix_lse.shape),
                pl.BlockSpec((1, width, depth), lambda t, core: (t * CORES + 1 - core[0], 0, 0)),
            ],
            out_specs=(out_spec, whole((rows, depth))),
            scratch_shapes=[
                pltpu.VMEM(ret.shape, jnp.float32),
                pltpu.VMEM((requests, PAD_ROWS, LANES), jnp.float32),
                pltpu.VMEM((requests, LANES), jnp.float32),
                pltpu.VMEM((requests * PAD_ROWS, LANES), jnp.float32),
            ],
        ),
        compiler_params=pltpu.CompilerParams(vmem_limit_bytes=VMEM_LIMIT),
        name="merge",
    )(core, codes, ret, suffix_out, suffix_lse, weights)
    received = lax.ppermute(other, "tensor", [(i, i ^ 1) for i in range(parts)])
    own = pl.pallas_call(
        project_kernel,
        out_shape=out_shape,
        grid_spec=pltpu.PrefetchScalarGridSpec(
            num_scalar_prefetch=1,
            grid=(parts // CORES,),
            in_specs=[
                whole((rows, depth)),
                pl.BlockSpec((1, width, depth), lambda t, core: (t * CORES + core[0], 0, 0)),
            ],
            out_specs=out_spec,
        ),
        compiler_params=pltpu.CompilerParams(vmem_limit_bytes=VMEM_LIMIT),
        cost_estimate=pl.CostEstimate(
            flops=2_000_000_000, bytes_accessed=2_000_000, transcendentals=0
        ),
        name="project",
    )(core, left, weights)
    return (own.astype(jnp.float32) + received.astype(jnp.float32)).astype(jnp.bfloat16)


def shards(queries, prefix_cache, suffix_cache, suffix_lengths, request_prefix, prefix_owner, out_proj):
    prefix_size = lax.axis_size("prefix")
    tensor_size = lax.axis_size("tensor")
    z_size = prefix_size // X_SIZE
    z_groups = [[z * X_SIZE + x for z in range(z_size)] for x in range(X_SIZE)]
    me = lax.axis_index("prefix").astype(jnp.int32).reshape(1)
    kv = prefix_cache[0, 0]
    q3 = queries.transpose(1, 0, 2)
    send, codes = route(me, request_prefix.reshape(-1), prefix_owner, q3, z_size)
    kv_out, send = lax.optimization_barrier((kv, send))

    def from_offset(array, offset):
        pairs = [
            (z * X_SIZE + (x + offset) % X_SIZE, z * X_SIZE + x)
            for z in range(z_size)
            for x in range(X_SIZE)
        ]
        return lax.ppermute(array, "prefix", pairs)

    right = from_offset(kv_out, 1)
    left = from_offset(kv_out, -1)
    opposite = from_offset(right, 1)
    recv = lax.all_to_all(
        send, "prefix", split_axis=0, concat_axis=0, axis_index_groups=z_groups, tiled=True
    )
    suffix_rows = suffix_cache[:, 0].transpose(0, 2, 1)
    suffix_out, suffix_lse = suffix_attention(suffix_lengths, q3, suffix_rows)
    recv, suffix_out, suffix_lse = lax.optimization_barrier((recv, suffix_out, suffix_lse))
    ret = prefix_attention(recv, (kv, right, left))
    ret = prefix_attention(recv, (opposite,), ret)
    homed = lax.all_to_all(
        ret, "prefix", split_axis=0, concat_axis=0, axis_index_groups=z_groups, tiled=True
    )
    core = (lax.axis_index("tensor").astype(jnp.int32) % CORES).reshape(1)
    parts = merge_project(core, codes, homed, suffix_out, suffix_lse, out_proj.T, tensor_size)
    y_groups = [[y * CORES + c for y in range(tensor_size // CORES)] for c in range(CORES)]
    parts = lax.all_to_all(
        parts, "tensor", split_axis=0, concat_axis=0, axis_index_groups=y_groups, tiled=True
    )
    parts = jnp.sum(parts.astype(jnp.float32), axis=0).astype(jnp.bfloat16)
    return parts.reshape(STEPS, queries.shape[0], -1).transpose(1, 0, 2)


def solution(mesh):
    return jax.shard_map(
        shards,
        mesh=mesh,
        in_specs=(
            P("prefix", None, "tensor"),
            P("prefix", "tensor", None, None),
            P("prefix", "tensor", None, None),
            P("prefix"),
            P(),
            P(),
            P("tensor", None),
        ),
        out_specs=P("prefix", None, "tensor"),
        check_vma=False,
    )
```

```python
import functools

import jax
import jax.numpy as jnp
from jax import lax
from jax.experimental import pallas as pl
from jax.experimental.pallas import tpu as pltpu
from jax.sharding import PartitionSpec as P

LANES = 128
HALF = 64
X_SIZE = 4
CORES = 2
CAPACITY = 2
GROUPS = X_SIZE * CAPACITY
STEPS = 3
ROWS = 12
PAD_ROWS = 16
SCALE = 0.125
VMEM_LIMIT = 56 * 1024 * 1024
SMALL_LIMIT = 32 * 1024 * 1024


def lane_iota(rows):
    return lax.broadcasted_iota(jnp.int32, (rows, LANES), 1)


def split_heads(rows):
    low = lane_iota(rows.shape[0]) < HALF
    even = jnp.where(low, rows, 0.0)
    odd = jnp.where(low, pltpu.roll(rows, HALF, 1), 0.0)
    return even, odd


def join_heads(even, odd):
    low = lane_iota(even.shape[0]) < HALF
    return jnp.where(low, pltpu.roll(even, HALF, 1), odd)


def nt_dot(left, right):
    return lax.dot_general(
        left, right, (((1,), (1,)), ((), ())), preferred_element_type=jnp.float32
    )


def spread_queries(q_ref, qs):
    requests = q_ref.shape[1]
    for i in range(PAD_ROWS):
        if i < ROWS:
            step, pair = divmod(i, ROWS // STEPS)
            value = q_ref[step, :, pair * LANES : (pair + 1) * LANES].astype(jnp.float32)
        else:
            value = jnp.zeros((requests, LANES), jnp.float32)
        qs[pl.ds(i, requests, stride=PAD_ROWS), :] = value


def route_kernel(me_ref, prefix_ref, owner_ref, q_ref, send_ref, code_ref, taken, source, qs, acc):
    requests = q_ref.shape[1]
    z_size = send_ref.shape[0]
    me = me_ref[0]
    x_own = me & (X_SIZE - 1)
    for i in range(owner_ref.shape[0]):
        taken[i] = 0
    for i in range(z_size * GROUPS):
        source[i] = 0

    def place(r, _):
        name = prefix_ref[me * requests + r]
        owner = owner_ref[name]
        rank = taken[name]
        taken[name] = rank + 1
        offset = (owner - x_own) & (X_SIZE - 1)
        code = (owner >> 2) * GROUPS + (offset ^ (offset >> 1)) * CAPACITY + rank
        code_ref[r] = code
        source[code] = r
        return 0

    lax.fori_loop(0, requests, place, 0, unroll=8)
    spread_queries(q_ref, qs)

    def fill(z, _):
        for slot in range(GROUPS):
            r = source[z * GROUPS + slot]
            block = qs[pl.ds(pl.multiple_of(r * PAD_ROWS, PAD_ROWS), PAD_ROWS), :]
            acc[z, slot * ROWS : (slot + 1) * ROWS, :] = block[:ROWS]
        return 0

    lax.fori_loop(0, z_size, fill, 0, unroll=4)
    send_ref[...] = acc[...].astype(jnp.bfloat16)


def route(me, prefixes, owner, q3, z_size):
    requests = q3.shape[1]
    smem = pl.BlockSpec(memory_space=pltpu.SMEM)
    vmem = pl.BlockSpec(memory_space=pltpu.VMEM)
    shape = (z_size, GROUPS * ROWS, LANES)
    return pl.pallas_call(
        route_kernel,
        out_shape=(
            jax.ShapeDtypeStruct(shape, jnp.bfloat16),
            jax.ShapeDtypeStruct((requests,), jnp.int32),
        ),
        in_specs=[smem, smem, smem, vmem],
        out_specs=(vmem, smem),
        scratch_shapes=[
            pltpu.SMEM((owner.shape[0],), jnp.int32),
            pltpu.SMEM((z_size * GROUPS,), jnp.int32),
            pltpu.VMEM((requests * PAD_ROWS, LANES), jnp.float32),
            pltpu.VMEM(shape, jnp.float32),
        ],
        compiler_params=pltpu.CompilerParams(vmem_limit_bytes=VMEM_LIMIT),
        name="route",
    )(me, prefixes, owner, q3)


SUFFIX_BLOCK = 4


def suffix_kernel(length_ref, q_ref, kv_ref, out_ref, lse_ref, qs):
    spread_queries(q_ref, qs)
    requests, positions, _ = kv_ref.shape
    rows = SUFFIX_BLOCK * PAD_ROWS
    shape = (2 * rows, SUFFIX_BLOCK * positions)
    row = lax.broadcasted_iota(jnp.int32, shape, 0) % rows
    request = row // PAD_ROWS
    step = row % PAD_ROWS // (ROWS // STEPS)
    place = lax.broadcasted_iota(jnp.int32, shape, 1) - request * positions
    past = jnp.where(place >= 0, place - step, 2 * positions)
    request_rows = lax.broadcasted_iota(jnp.int32, (2 * rows, 1), 0) % rows // PAD_ROWS
    low = lane_iota(rows) < HALF

    def some(i, _):
        here = pl.ds(pl.multiple_of(i * rows, rows), rows)
        even, odd = split_heads(qs[here, :] * SCALE)
        query = jnp.concatenate([even, odd], axis=0).astype(jnp.bfloat16)
        cache = kv_ref[pl.ds(i * SUFFIX_BLOCK, SUFFIX_BLOCK)].reshape(-1, LANES)
        limit = jnp.zeros((2 * rows, 1), jnp.int32)
        for r in range(SUFFIX_BLOCK):
            limit = jnp.where(request_rows == r, length_ref[i * SUFFIX_BLOCK + r] - (STEPS - 1), limit)
        scores = jnp.where(past < limit, nt_dot(query, cache), -jnp.inf)
        highest = jnp.max(scores, axis=1, keepdims=True)
        weight = jnp.exp(scores - highest)
        total = jnp.sum(weight, axis=1, keepdims=True)
        mixed = jnp.dot(weight.astype(jnp.bfloat16), cache, preferred_element_type=jnp.float32)
        mixed = mixed / total
        lse = highest + jnp.log(total)
        out_ref[here, :] = join_heads(mixed[:rows], mixed[rows:])
        lse_ref[here, :] = jnp.where(low, lse[:rows], lse[rows:])
        return 0

    lax.fori_loop(0, requests // SUFFIX_BLOCK, some, 0, unroll=2)


def suffix_attention(lengths, q3, kv):
    requests = kv.shape[0]
    vmem = pl.BlockSpec(memory_space=pltpu.VMEM)
    shape = jax.ShapeDtypeStruct((requests * PAD_ROWS, LANES), jnp.float32)
    return pl.pallas_call(
        suffix_kernel,
        out_shape=(shape, shape),
        in_specs=[pl.BlockSpec(memory_space=pltpu.SMEM), vmem, vmem],
        out_specs=(vmem, vmem),
        scratch_shapes=[pltpu.VMEM((requests * PAD_ROWS, LANES), jnp.float32)],
        compiler_params=pltpu.CompilerParams(vmem_limit_bytes=VMEM_LIMIT),
        cost_estimate=pl.CostEstimate(
            flops=8_000_000_000, bytes_accessed=8_000_000, transcendentals=0
        ),
        name="suffix",
    )(lengths, q3, kv)


CHUNKS = 2


def prefix_kernel(count, start, recv_ref, *refs):
    sources = refs[: len(refs) - 8]
    ret_ref, cache, values, queries, acc, stage_out, sems, out_sem = refs[-8:]
    index = pl.program_id(0)
    z_size = recv_ref.shape[0]
    span = CAPACITY * ROWS
    rows = z_size * span
    copies = [pltpu.make_async_copy(sources[i], cache.at[i], sems.at[i]) for i in range(count)]

    @pl.when(index == 0)
    def _():
        for copy in copies:
            copy.start()
        queries[...] = recv_ref[...].astype(jnp.float32) * SCALE
        values[HALF:, :] = jnp.ones_like(values[HALF:, :])
        acc[...] = jnp.zeros_like(acc)

    group = index + (X_SIZE - count if start else 0)
    for i in range(count):
        pl.when(index == i)(copies[i].wait)
    values[:HALF, :] = cache[index, HALF:]
    place = pl.ds(pl.multiple_of(group * span, 8), span)
    own_place = pl.ds(pl.multiple_of(index * span, 8), span)
    query = jnp.concatenate(split_heads(queries[:, place, :].reshape(rows, LANES)), axis=0)
    query = query.astype(jnp.bfloat16)
    size = 2 * rows // CHUNKS
    scores, weights, mixes = [None] * CHUNKS, [None] * CHUNKS, []
    for stage in range(CHUNKS + 2):
        if stage < CHUNKS:
            here = query[stage * size : (stage + 1) * size]
            scores[stage] = jnp.dot(here, cache[index], preferred_element_type=jnp.float32)
        if stage >= 2:
            weight, highest = weights[stage - 2]
            mixed = nt_dot(weight, values[...])
            low = lane_iota(size) < HALF
            total = jnp.where(low, pltpu.roll(mixed, HALF, 1), mixed)
            mixes.append((mixed / total, highest + jnp.log(total)))
        if 1 <= stage <= CHUNKS:
            highest = jnp.max(scores[stage - 1], axis=1, keepdims=True)
            weight = jnp.exp(scores[stage - 1] - highest).astype(jnp.bfloat16)
            weights[stage - 1] = (weight, highest)
    half = CHUNKS // 2
    low = lane_iota(size) < HALF
    lse = []
    for i in range(half):
        out = jnp.where(low, mixes[i][0], pltpu.roll(mixes[i + half][0], HALF, 1))
        sources = slice(i * z_size // half, (i + 1) * z_size // half)
        acc[sources, own_place, :] = out.reshape(z_size // half, span, LANES)
        lse.append(jnp.where(low, mixes[i][1], mixes[i + half][1]))
    lse = jnp.concatenate(lse, axis=0)
    lane = lax.broadcasted_iota(jnp.int32, (span, LANES), 1) & (HALF - 1)
    row = lax.broadcasted_iota(jnp.int32, (span, LANES), 0)
    row = jnp.where(row < ROWS, row, row - ROWS)
    high_part = lse.astype(jnp.bfloat16).astype(jnp.float32)
    rest = lse - high_part
    mid_part = rest.astype(jnp.bfloat16).astype(jnp.float32)
    packed = jnp.zeros((z_size, span, LANES), jnp.float32)
    for i, part in enumerate((high_part, mid_part, rest - mid_part)):
        part = part.reshape(z_size, span, LANES)
        packed = jnp.where((lane == row + i * ROWS)[None], part, packed)
    packed = packed.reshape(rows, LANES).astype(jnp.bfloat16)
    shape = (z_size * GROUPS, rows)
    slot = lax.broadcasted_iota(jnp.int32, shape, 0)
    inside = (slot & (GROUPS - 1)) // CAPACITY == index
    slot = slot // GROUPS * CAPACITY + (slot & (CAPACITY - 1))
    first = lax.broadcasted_iota(jnp.int32, shape, 1) - slot * ROWS
    pick = jnp.logical_and(inside, jnp.logical_and(first >= 0, first < ROWS))
    lse_rows = jnp.dot(pick.astype(jnp.bfloat16), packed, preferred_element_type=jnp.float32)
    lse_rows = lse_rows.reshape(z_size, GROUPS, LANES)
    own = lax.broadcasted_iota(jnp.int32, (GROUPS, LANES), 0) // CAPACITY == index
    acc[:, count * span :, :] = jnp.where(own[None], lse_rows, acc[:, count * span :, :])

    @pl.when(index == count - 1)
    def _():
        stage_out[...] = acc[...].astype(jnp.bfloat16)
        copy = pltpu.make_async_copy(
            stage_out, ret_ref.at[:, start : start + stage_out.shape[1], :], out_sem
        )
        copy.start()
        copy.wait()


FIRST_GROUPS = 3
FIRST_ROWS = FIRST_GROUPS * CAPACITY * ROWS + GROUPS
ALL_ROWS = FIRST_ROWS + CAPACITY * ROWS + GROUPS


def prefix_attention(recv, caches, before=None):
    z_size = recv.shape[0]
    count = len(caches)
    start = 0 if before is None else FIRST_ROWS
    length = caches[0].shape[1]
    rows = count * CAPACITY * ROWS + GROUPS
    vmem = pl.BlockSpec(memory_space=pltpu.VMEM)
    anywhere = pl.BlockSpec(memory_space=pl.ANY)
    kernel = functools.partial(prefix_kernel, count, start)
    operands = [recv, *caches]
    aliases = {}
    if before is not None:
        aliases = {len(operands): 0}
        operands.append(before)
        inner = kernel
        kernel = lambda *refs: inner(*refs[:2], *refs[3:])
    return pl.pallas_call(
        kernel,
        grid=(count,),
        out_shape=jax.ShapeDtypeStruct((z_size, ALL_ROWS, LANES), jnp.bfloat16),
        in_specs=[vmem] + [anywhere] * (len(operands) - 1),
        out_specs=anywhere,
        scratch_shapes=[
            pltpu.VMEM((count, LANES, length), jnp.bfloat16),
            pltpu.VMEM((LANES, length), jnp.bfloat16),
            pltpu.VMEM(recv.shape, jnp.float32),
            pltpu.VMEM((z_size, rows, LANES), jnp.float32),
            pltpu.VMEM((z_size, rows, LANES), jnp.bfloat16),
            pltpu.SemaphoreType.DMA((count,)),
            pltpu.SemaphoreType.DMA,
        ],
        input_output_aliases=aliases,
        compiler_params=pltpu.CompilerParams(vmem_limit_bytes=SMALL_LIMIT),
        cost_estimate=pl.CostEstimate(
            flops=2_500_000_000 * count, bytes_accessed=1_000_000 * count, transcendentals=0
        ),
        name="prefix",
    )(*operands)


def merge_kernel(core_ref, code_ref, ret_ref, suffix_ref, suffix_lse_ref, w_ref, out_ref, left, wide, picked, packed, merged):
    requests = code_ref.shape[0]

    @pl.when(pl.program_id(0) == 0)
    def _():
        wide[...] = ret_ref[...].astype(jnp.float32)
        pair_rows = CAPACITY * ROWS
        for r in range(requests):
            code = code_ref[r]
            z, slot = code // GROUPS, code % GROUPS
            group = slot // CAPACITY
            last = group == FIRST_GROUPS
            start = pl.multiple_of(jnp.where(last, FIRST_ROWS, group * pair_rows), 8)
            lse_row = slot + jnp.where(
                last, ALL_ROWS - GROUPS - FIRST_GROUPS * CAPACITY, FIRST_ROWS - GROUPS
            )
            pair = wide[z, pl.ds(start, pair_rows), :]
            second = jnp.concatenate([pair[ROWS:], pair[: PAD_ROWS - ROWS]], axis=0)
            picked[r] = jnp.where(slot % CAPACITY == 0, pair[:PAD_ROWS], second)
            packed[r : r + 1, :] = wide[z, pl.ds(lse_row, 1), :]
        lane = lane_iota(PAD_ROWS) % HALF
        row = lax.broadcasted_iota(jnp.int32, (PAD_ROWS, LANES), 0)
        own = jnp.logical_or(lane == row, jnp.logical_or(lane == row + ROWS, lane == row + 2 * ROWS))
        own = jnp.logical_and(own, row < ROWS)
        copies = jnp.where(own[None], packed[...][:, None, :], 0.0).astype(jnp.bfloat16)
        same_half = lax.broadcasted_iota(jnp.int32, (LANES, LANES), 0) // HALF
        same_half = same_half == lane_iota(LANES) // HALF
        prefix_lse = jnp.dot(
            copies.reshape(requests * PAD_ROWS, LANES),
            same_half.astype(jnp.bfloat16),
            preferred_element_type=jnp.float32,
        )
        gap = prefix_lse - suffix_lse_ref[...]
        small = jnp.exp(-jnp.abs(gap))
        large_weight = 1.0 / (1.0 + small)
        small_weight = small * large_weight
        prefix_first = gap >= 0.0
        merged[...] = picked[...].reshape(requests * PAD_ROWS, LANES) * jnp.where(
            prefix_first, large_weight, small_weight
        ) + suffix_ref[...] * jnp.where(prefix_first, small_weight, large_weight)
        pairs = ROWS // STEPS
        for step in range(STEPS):
            for pair in range(pairs):
                left[step * requests : (step + 1) * requests, pair * LANES : (pair + 1) * LANES] = merged[
                    pl.ds(step * pairs + pair, requests, stride=PAD_ROWS), :
                ].astype(jnp.bfloat16)

    for part in range(w_ref.shape[0]):
        out_ref[part] = nt_dot(left[...], w_ref[part, 0]).astype(jnp.bfloat16)


def project_kernel(core_ref, left_ref, w_ref, out_ref):
    for part in range(w_ref.shape[0]):
        out_ref[part] = nt_dot(left_ref[...], w_ref[part, core_ref[0]]).astype(jnp.bfloat16)


def merge_project(core, codes, ret, suffix_out, suffix_lse, weights, parts):
    requests = codes.shape[0]
    width = weights.shape[0] // parts
    depth = weights.shape[1]
    rows = STEPS * requests
    weights = weights.reshape(parts // CORES, CORES, width, depth)
    whole = lambda shape: pl.BlockSpec(shape, lambda t, core: (0,) * len(shape))
    out_spec = whole((parts // CORES, rows, width))
    out_shape = jax.ShapeDtypeStruct((parts // CORES, rows, width), jnp.bfloat16)
    other, left = pl.pallas_call(
        merge_kernel,
        out_shape=(out_shape, jax.ShapeDtypeStruct((rows, depth), jnp.bfloat16)),
        grid_spec=pltpu.PrefetchScalarGridSpec(
            num_scalar_prefetch=1,
            grid=(1,),
            in_specs=[
                pl.BlockSpec(memory_space=pltpu.SMEM),
                whole(ret.shape),
                whole(suffix_out.shape),
                whole(suffix_lse.shape),
                pl.BlockSpec((parts // CORES, 1, width, depth), lambda t, core: (0, 1 - core[0], 0, 0)),
            ],
            out_specs=(out_spec, whole((rows, depth))),
            scratch_shapes=[
                pltpu.VMEM(ret.shape, jnp.float32),
                pltpu.VMEM((requests, PAD_ROWS, LANES), jnp.float32),
                pltpu.VMEM((requests, LANES), jnp.float32),
                pltpu.VMEM((requests * PAD_ROWS, LANES), jnp.float32),
            ],
        ),
        compiler_params=pltpu.CompilerParams(vmem_limit_bytes=VMEM_LIMIT),
        name="merge",
    )(core, codes, ret, suffix_out, suffix_lse, weights)
    received = lax.ppermute(other, "tensor", [(i, i ^ 1) for i in range(parts)])
    vmem = pl.BlockSpec(memory_space=pltpu.VMEM)
    own = pl.pallas_call(
        project_kernel,
        out_shape=out_shape,
        in_specs=[pl.BlockSpec(memory_space=pltpu.SMEM), vmem, vmem],
        out_specs=vmem,
        compiler_params=pltpu.CompilerParams(vmem_limit_bytes=SMALL_LIMIT),
        cost_estimate=pl.CostEstimate(
            flops=2_000_000_000, bytes_accessed=2_000_000, transcendentals=0
        ),
        name="project",
    )(core, left, weights)
    return (own.astype(jnp.float32) + received.astype(jnp.float32)).astype(jnp.bfloat16)


def shards(queries, prefix_cache, suffix_cache, suffix_lengths, request_prefix, prefix_owner, out_proj):
    prefix_size = lax.axis_size("prefix")
    tensor_size = lax.axis_size("tensor")
    z_size = prefix_size // X_SIZE
    z_groups = [[z * X_SIZE + x for z in range(z_size)] for x in range(X_SIZE)]
    me = lax.axis_index("prefix").astype(jnp.int32).reshape(1)
    kv = prefix_cache[0, 0]
    q3 = queries.transpose(1, 0, 2)
    send, codes = route(me, request_prefix.reshape(-1), prefix_owner, q3, z_size)
    kv_out, send = lax.optimization_barrier((kv, send))

    def from_offset(array, offset):
        pairs = [
            (z * X_SIZE + (x + offset) % X_SIZE, z * X_SIZE + x)
            for z in range(z_size)
            for x in range(X_SIZE)
        ]
        return lax.ppermute(array, "prefix", pairs)

    right = from_offset(kv, 1)
    left = from_offset(kv_out, -1)
    opposite = from_offset(right, 1)
    recv = lax.all_to_all(
        send, "prefix", split_axis=0, concat_axis=0, axis_index_groups=z_groups, tiled=True
    )
    suffix_rows = suffix_cache[:, 0].transpose(0, 2, 1)
    suffix_out, suffix_lse = suffix_attention(suffix_lengths, q3, suffix_rows)
    recv, suffix_out, suffix_lse = lax.optimization_barrier((recv, suffix_out, suffix_lse))
    ret = prefix_attention(recv, (kv, right, left))
    ret = prefix_attention(recv, (opposite,), ret)
    homed = lax.all_to_all(
        ret, "prefix", split_axis=0, concat_axis=0, axis_index_groups=z_groups, tiled=True
    )
    core = (lax.axis_index("tensor").astype(jnp.int32) % CORES).reshape(1)
    parts = merge_project(core, codes, homed, suffix_out, suffix_lse, out_proj.T, tensor_size)
    y_groups = [[y * CORES + c for y in range(tensor_size // CORES)] for c in range(CORES)]
    parts = lax.all_to_all(
        parts, "tensor", split_axis=0, concat_axis=0, axis_index_groups=y_groups, tiled=True
    )
    parts = jnp.sum(parts.astype(jnp.float32), axis=0).astype(jnp.bfloat16)
    return parts.reshape(STEPS, queries.shape[0], -1).transpose(1, 0, 2)


def solution(mesh):
    return jax.shard_map(
        shards,
        mesh=mesh,
        in_specs=(
            P("prefix", None, "tensor"),
            P("prefix", "tensor", None, None),
            P("prefix", "tensor", None, None),
            P("prefix"),
            P(),
            P(),
            P("tensor", None),
        ),
        out_specs=P("prefix", None, "tensor"),
        check_vma=False,
    )
```

```python
import functools

import jax
import jax.numpy as jnp
from jax import lax
from jax.experimental import pallas as pl
from jax.experimental.pallas import tpu as pltpu
from jax.sharding import PartitionSpec as P

LANES = 128
HALF = 64
X_SIZE = 4
CORES = 2
CAPACITY = 2
GROUPS = X_SIZE * CAPACITY
STEPS = 3
ROWS = 12
PAD_ROWS = 16
SCALE = 0.125
VMEM_LIMIT = 56 * 1024 * 1024
SMALL_LIMIT = 32 * 1024 * 1024
MERGE_LIMIT = 52 * 1024 * 1024


def lane_iota(rows):
    return lax.broadcasted_iota(jnp.int32, (rows, LANES), 1)


def split_heads(rows):
    low = lane_iota(rows.shape[0]) < HALF
    even = jnp.where(low, rows, 0.0)
    odd = jnp.where(low, pltpu.roll(rows, HALF, 1), 0.0)
    return even, odd


def join_heads(even, odd):
    low = lane_iota(even.shape[0]) < HALF
    return jnp.where(low, pltpu.roll(even, HALF, 1), odd)


def nt_dot(left, right):
    return lax.dot_general(
        left, right, (((1,), (1,)), ((), ())), preferred_element_type=jnp.float32
    )


def spread_queries(q_ref, qs):
    requests = q_ref.shape[1]
    for i in range(PAD_ROWS):
        if i < ROWS:
            step, pair = divmod(i, ROWS // STEPS)
            value = q_ref[step, :, pair * LANES : (pair + 1) * LANES].astype(jnp.float32)
        else:
            value = jnp.zeros((requests, LANES), jnp.float32)
        qs[pl.ds(i, requests, stride=PAD_ROWS), :] = value


def route_kernel(me_ref, prefix_ref, owner_ref, q_ref, send_ref, code_ref, taken, source, qs, acc):
    requests = q_ref.shape[1]
    z_size = send_ref.shape[0]
    me = me_ref[0]
    x_own = me & (X_SIZE - 1)
    for i in range(owner_ref.shape[0]):
        taken[i] = 0
    for i in range(z_size * GROUPS):
        source[i] = 0

    def place(r, _):
        name = prefix_ref[me * requests + r]
        owner = owner_ref[name]
        rank = taken[name]
        taken[name] = rank + 1
        offset = (owner - x_own) & (X_SIZE - 1)
        code = (owner >> 2) * GROUPS + (offset ^ (offset >> 1)) * CAPACITY + rank
        code_ref[r] = code
        source[code] = r
        return 0

    lax.fori_loop(0, requests, place, 0, unroll=8)
    spread_queries(q_ref, qs)

    def fill(z, _):
        for slot in range(GROUPS):
            r = source[z * GROUPS + slot]
            block = qs[pl.ds(pl.multiple_of(r * PAD_ROWS, PAD_ROWS), PAD_ROWS), :]
            acc[z, slot * ROWS : (slot + 1) * ROWS, :] = block[:ROWS]
        return 0

    lax.fori_loop(0, z_size, fill, 0, unroll=4)
    send_ref[...] = acc[...].astype(jnp.bfloat16)


def route(me, prefixes, owner, q3, z_size):
    requests = q3.shape[1]
    smem = pl.BlockSpec(memory_space=pltpu.SMEM)
    vmem = pl.BlockSpec(memory_space=pltpu.VMEM)
    shape = (z_size, GROUPS * ROWS, LANES)
    return pl.pallas_call(
        route_kernel,
        out_shape=(
            jax.ShapeDtypeStruct(shape, jnp.bfloat16),
            jax.ShapeDtypeStruct((requests,), jnp.int32),
        ),
        in_specs=[smem, smem, smem, vmem],
        out_specs=(vmem, smem),
        scratch_shapes=[
            pltpu.SMEM((owner.shape[0],), jnp.int32),
            pltpu.SMEM((z_size * GROUPS,), jnp.int32),
            pltpu.VMEM((requests * PAD_ROWS, LANES), jnp.float32),
            pltpu.VMEM(shape, jnp.float32),
        ],
        compiler_params=pltpu.CompilerParams(vmem_limit_bytes=VMEM_LIMIT),
        name="route",
    )(me, prefixes, owner, q3)


SUFFIX_BLOCK = 4


def suffix_kernel(length_ref, q_ref, kv_ref, out_ref, lse_ref, qs):
    spread_queries(q_ref, qs)
    requests, positions, _ = kv_ref.shape
    rows = SUFFIX_BLOCK * PAD_ROWS
    shape = (2 * rows, SUFFIX_BLOCK * positions)
    row = lax.broadcasted_iota(jnp.int32, shape, 0) % rows
    request = row // PAD_ROWS
    step = row % PAD_ROWS // (ROWS // STEPS)
    place = lax.broadcasted_iota(jnp.int32, shape, 1) - request * positions
    past = jnp.where(place >= 0, place - step, 2 * positions)
    request_rows = lax.broadcasted_iota(jnp.int32, (2 * rows, 1), 0) % rows // PAD_ROWS
    low = lane_iota(rows) < HALF

    def some(i, _):
        here = pl.ds(pl.multiple_of(i * rows, rows), rows)
        even, odd = split_heads(qs[here, :] * SCALE)
        query = jnp.concatenate([even, odd], axis=0).astype(jnp.bfloat16)
        cache = kv_ref[pl.ds(i * SUFFIX_BLOCK, SUFFIX_BLOCK)].reshape(-1, LANES)
        limit = jnp.zeros((2 * rows, 1), jnp.int32)
        for r in range(SUFFIX_BLOCK):
            limit = jnp.where(request_rows == r, length_ref[i * SUFFIX_BLOCK + r] - (STEPS - 1), limit)
        scores = jnp.where(past < limit, nt_dot(query, cache), -jnp.inf)
        highest = jnp.max(scores, axis=1, keepdims=True)
        weight = jnp.exp(scores - highest)
        total = jnp.sum(weight, axis=1, keepdims=True)
        mixed = jnp.dot(weight.astype(jnp.bfloat16), cache, preferred_element_type=jnp.float32)
        mixed = mixed / total
        lse = highest + jnp.log(total)
        out_ref[here, :] = join_heads(mixed[:rows], mixed[rows:])
        lse_ref[here, :] = jnp.where(low, lse[:rows], lse[rows:])
        return 0

    lax.fori_loop(0, requests // SUFFIX_BLOCK, some, 0, unroll=2)


def suffix_attention(lengths, q3, kv):
    requests = kv.shape[0]
    vmem = pl.BlockSpec(memory_space=pltpu.VMEM)
    shape = jax.ShapeDtypeStruct((requests * PAD_ROWS, LANES), jnp.float32)
    return pl.pallas_call(
        suffix_kernel,
        out_shape=(shape, shape),
        in_specs=[pl.BlockSpec(memory_space=pltpu.SMEM), vmem, vmem],
        out_specs=(vmem, vmem),
        scratch_shapes=[pltpu.VMEM((requests * PAD_ROWS, LANES), jnp.float32)],
        compiler_params=pltpu.CompilerParams(vmem_limit_bytes=VMEM_LIMIT),
        cost_estimate=pl.CostEstimate(
            flops=8_000_000_000, bytes_accessed=8_000_000, transcendentals=0
        ),
        name="suffix",
    )(lengths, q3, kv)


CHUNKS = 2


def prefix_kernel(count, start, recv_ref, *refs):
    sources = refs[: len(refs) - 8]
    ret_ref, cache, values, queries, acc, stage_out, sems, out_sem = refs[-8:]
    index = pl.program_id(0)
    z_size = recv_ref.shape[0]
    span = CAPACITY * ROWS
    rows = z_size * span
    copies = [pltpu.make_async_copy(sources[i], cache.at[i], sems.at[i]) for i in range(count)]

    @pl.when(index == 0)
    def _():
        for copy in copies:
            copy.start()
        queries[...] = recv_ref[...].astype(jnp.float32) * SCALE
        values[HALF:, :] = jnp.ones_like(values[HALF:, :])
        acc[...] = jnp.zeros_like(acc)

    group = index + (X_SIZE - count if start else 0)
    for i in range(count):
        pl.when(index == i)(copies[i].wait)
    values[:HALF, :] = cache[index, HALF:]
    place = pl.ds(pl.multiple_of(group * span, 8), span)
    own_place = pl.ds(pl.multiple_of(index * span, 8), span)
    query = jnp.concatenate(split_heads(queries[:, place, :].reshape(rows, LANES)), axis=0)
    query = query.astype(jnp.bfloat16)
    size = 2 * rows // CHUNKS
    scores, weights, mixes = [None] * CHUNKS, [None] * CHUNKS, []
    for stage in range(CHUNKS + 2):
        if stage < CHUNKS:
            here = query[stage * size : (stage + 1) * size]
            scores[stage] = jnp.dot(here, cache[index], preferred_element_type=jnp.float32)
        if stage >= 2:
            weight, highest = weights[stage - 2]
            mixed = nt_dot(weight, values[...])
            low = lane_iota(size) < HALF
            total = jnp.where(low, pltpu.roll(mixed, HALF, 1), mixed)
            mixes.append((mixed / total, highest + jnp.log(total)))
        if 1 <= stage <= CHUNKS:
            highest = jnp.max(scores[stage - 1], axis=1, keepdims=True)
            weight = jnp.exp(scores[stage - 1] - highest).astype(jnp.bfloat16)
            weights[stage - 1] = (weight, highest)
    half = CHUNKS // 2
    low = lane_iota(size) < HALF
    lse = []
    for i in range(half):
        out = jnp.where(low, mixes[i][0], pltpu.roll(mixes[i + half][0], HALF, 1))
        sources = slice(i * z_size // half, (i + 1) * z_size // half)
        acc[sources, own_place, :] = out.reshape(z_size // half, span, LANES)
        lse.append(jnp.where(low, mixes[i][1], mixes[i + half][1]))
    lse = jnp.concatenate(lse, axis=0)
    lane = lax.broadcasted_iota(jnp.int32, (span, LANES), 1) & (HALF - 1)
    row = lax.broadcasted_iota(jnp.int32, (span, LANES), 0)
    row = jnp.where(row < ROWS, row, row - ROWS)
    high_part = lse.astype(jnp.bfloat16).astype(jnp.float32)
    rest = lse - high_part
    mid_part = rest.astype(jnp.bfloat16).astype(jnp.float32)
    packed = jnp.zeros((z_size, span, LANES), jnp.float32)
    for i, part in enumerate((high_part, mid_part, rest - mid_part)):
        part = part.reshape(z_size, span, LANES)
        packed = jnp.where((lane == row + i * ROWS)[None], part, packed)
    packed = packed.reshape(rows, LANES).astype(jnp.bfloat16)
    shape = (z_size * GROUPS, rows)
    slot = lax.broadcasted_iota(jnp.int32, shape, 0)
    inside = (slot & (GROUPS - 1)) // CAPACITY == index
    slot = slot // GROUPS * CAPACITY + (slot & (CAPACITY - 1))
    first = lax.broadcasted_iota(jnp.int32, shape, 1) - slot * ROWS
    pick = jnp.logical_and(inside, jnp.logical_and(first >= 0, first < ROWS))
    lse_rows = jnp.dot(pick.astype(jnp.bfloat16), packed, preferred_element_type=jnp.float32)
    lse_rows = lse_rows.reshape(z_size, GROUPS, LANES)
    own = lax.broadcasted_iota(jnp.int32, (GROUPS, LANES), 0) // CAPACITY == index
    acc[:, count * span :, :] = jnp.where(own[None], lse_rows, acc[:, count * span :, :])

    @pl.when(index == count - 1)
    def _():
        stage_out[...] = acc[...].astype(jnp.bfloat16)
        copy = pltpu.make_async_copy(
            stage_out, ret_ref.at[:, start : start + stage_out.shape[1], :], out_sem
        )
        copy.start()
        copy.wait()


FIRST_GROUPS = 3
FIRST_ROWS = FIRST_GROUPS * CAPACITY * ROWS + GROUPS
ALL_ROWS = FIRST_ROWS + CAPACITY * ROWS + GROUPS


def prefix_attention(recv, caches, before=None):
    z_size = recv.shape[0]
    count = len(caches)
    start = 0 if before is None else FIRST_ROWS
    length = caches[0].shape[1]
    rows = count * CAPACITY * ROWS + GROUPS
    vmem = pl.BlockSpec(memory_space=pltpu.VMEM)
    anywhere = pl.BlockSpec(memory_space=pl.ANY)
    kernel = functools.partial(prefix_kernel, count, start)
    operands = [recv, *caches]
    aliases = {}
    if before is not None:
        aliases = {len(operands): 0}
        operands.append(before)
        inner = kernel
        kernel = lambda *refs: inner(*refs[:2], *refs[3:])
    return pl.pallas_call(
        kernel,
        grid=(count,),
        out_shape=jax.ShapeDtypeStruct((z_size, ALL_ROWS, LANES), jnp.bfloat16),
        in_specs=[vmem] + [anywhere] * (len(operands) - 1),
        out_specs=anywhere,
        scratch_shapes=[
            pltpu.VMEM((count, LANES, length), jnp.bfloat16),
            pltpu.VMEM((LANES, length), jnp.bfloat16),
            pltpu.VMEM(recv.shape, jnp.float32),
            pltpu.VMEM((z_size, rows, LANES), jnp.float32),
            pltpu.VMEM((z_size, rows, LANES), jnp.bfloat16),
            pltpu.SemaphoreType.DMA((count,)),
            pltpu.SemaphoreType.DMA,
        ],
        input_output_aliases=aliases,
        compiler_params=pltpu.CompilerParams(vmem_limit_bytes=SMALL_LIMIT),
        cost_estimate=pl.CostEstimate(
            flops=2_500_000_000 * count, bytes_accessed=1_000_000 * count, transcendentals=0
        ),
        name="prefix",
    )(*operands)


def merge_kernel(core_ref, code_ref, ret_ref, suffix_ref, suffix_lse_ref, w_ref, out_ref, left, wide, picked, packed, merged):
    requests = code_ref.shape[0]

    @pl.when(pl.program_id(0) == 0)
    def _():
        wide[...] = ret_ref[...].astype(jnp.float32)
        pair_rows = CAPACITY * ROWS
        for r in range(requests):
            code = code_ref[r]
            z, slot = code // GROUPS, code % GROUPS
            group = slot // CAPACITY
            last = group == FIRST_GROUPS
            start = pl.multiple_of(jnp.where(last, FIRST_ROWS, group * pair_rows), 8)
            lse_row = slot + jnp.where(
                last, ALL_ROWS - GROUPS - FIRST_GROUPS * CAPACITY, FIRST_ROWS - GROUPS
            )
            pair = wide[z, pl.ds(start, pair_rows), :]
            second = jnp.concatenate([pair[ROWS:], pair[: PAD_ROWS - ROWS]], axis=0)
            picked[r] = jnp.where(slot % CAPACITY == 0, pair[:PAD_ROWS], second)
            packed[r : r + 1, :] = wide[z, pl.ds(lse_row, 1), :]
        lane = lane_iota(PAD_ROWS) % HALF
        row = lax.broadcasted_iota(jnp.int32, (PAD_ROWS, LANES), 0)
        own = jnp.logical_or(lane == row, jnp.logical_or(lane == row + ROWS, lane == row + 2 * ROWS))
        own = jnp.logical_and(own, row < ROWS)
        copies = jnp.where(own[None], packed[...][:, None, :], 0.0).astype(jnp.bfloat16)
        same_half = lax.broadcasted_iota(jnp.int32, (LANES, LANES), 0) // HALF
        same_half = same_half == lane_iota(LANES) // HALF
        prefix_lse = jnp.dot(
            copies.reshape(requests * PAD_ROWS, LANES),
            same_half.astype(jnp.bfloat16),
            preferred_element_type=jnp.float32,
        )
        gap = prefix_lse - suffix_lse_ref[...]
        small = jnp.exp(-jnp.abs(gap))
        large_weight = 1.0 / (1.0 + small)
        small_weight = small * large_weight
        prefix_first = gap >= 0.0
        merged[...] = picked[...].reshape(requests * PAD_ROWS, LANES) * jnp.where(
            prefix_first, large_weight, small_weight
        ) + suffix_ref[...] * jnp.where(prefix_first, small_weight, large_weight)
        pairs = ROWS // STEPS
        for step in range(STEPS):
            for pair in range(pairs):
                left[step * requests : (step + 1) * requests, pair * LANES : (pair + 1) * LANES] = merged[
                    pl.ds(step * pairs + pair, requests, stride=PAD_ROWS), :
                ].astype(jnp.bfloat16)

    for part in range(w_ref.shape[0]):
        out_ref[part] = nt_dot(left[...], w_ref[part, 0]).astype(jnp.bfloat16)


def project_kernel(core_ref, left_ref, w_ref, out_ref):
    for part in range(w_ref.shape[0]):
        out_ref[part] = nt_dot(left_ref[...], w_ref[part, core_ref[0]]).astype(jnp.bfloat16)


def merge_project(core, codes, ret, suffix_out, suffix_lse, weights, parts):
    requests = codes.shape[0]
    width = weights.shape[0] // parts
    depth = weights.shape[1]
    rows = STEPS * requests
    weights = weights.reshape(parts // CORES, CORES, width, depth)
    whole = lambda shape: pl.BlockSpec(shape, lambda t, core: (0,) * len(shape))
    out_spec = whole((parts // CORES, rows, width))
    out_shape = jax.ShapeDtypeStruct((parts // CORES, rows, width), jnp.bfloat16)
    other, left = pl.pallas_call(
        merge_kernel,
        out_shape=(out_shape, jax.ShapeDtypeStruct((rows, depth), jnp.bfloat16)),
        grid_spec=pltpu.PrefetchScalarGridSpec(
            num_scalar_prefetch=1,
            grid=(1,),
            in_specs=[
                pl.BlockSpec(memory_space=pltpu.SMEM),
                whole(ret.shape),
                whole(suffix_out.shape),
                whole(suffix_lse.shape),
                pl.BlockSpec((parts // CORES, 1, width, depth), lambda t, core: (0, 1 - core[0], 0, 0)),
            ],
            out_specs=(out_spec, whole((rows, depth))),
            scratch_shapes=[
                pltpu.VMEM(ret.shape, jnp.float32),
                pltpu.VMEM((requests, PAD_ROWS, LANES), jnp.float32),
                pltpu.VMEM((requests, LANES), jnp.float32),
                pltpu.VMEM((requests * PAD_ROWS, LANES), jnp.float32),
            ],
        ),
        compiler_params=pltpu.CompilerParams(vmem_limit_bytes=MERGE_LIMIT),
        name="merge",
    )(core, codes, ret, suffix_out, suffix_lse, weights)
    received = lax.ppermute(other, "tensor", [(i, i ^ 1) for i in range(parts)])
    vmem = pl.BlockSpec(memory_space=pltpu.VMEM)
    own = pl.pallas_call(
        project_kernel,
        out_shape=out_shape,
        in_specs=[pl.BlockSpec(memory_space=pltpu.SMEM), vmem, vmem],
        out_specs=vmem,
        compiler_params=pltpu.CompilerParams(vmem_limit_bytes=SMALL_LIMIT),
        cost_estimate=pl.CostEstimate(
            flops=2_000_000_000, bytes_accessed=2_000_000, transcendentals=0
        ),
        name="project",
    )(core, left, weights)
    return (own.astype(jnp.float32) + received.astype(jnp.float32)).astype(jnp.bfloat16)


def shards(queries, prefix_cache, suffix_cache, suffix_lengths, request_prefix, prefix_owner, out_proj):
    prefix_size = lax.axis_size("prefix")
    tensor_size = lax.axis_size("tensor")
    z_size = prefix_size // X_SIZE
    z_groups = [[z * X_SIZE + x for z in range(z_size)] for x in range(X_SIZE)]
    me = lax.axis_index("prefix").astype(jnp.int32).reshape(1)
    kv = prefix_cache[0, 0]
    q3 = queries.transpose(1, 0, 2)
    send, codes = route(me, request_prefix.reshape(-1), prefix_owner, q3, z_size)
    kv_out, send = lax.optimization_barrier((kv, send))

    def from_offset(array, offset):
        pairs = [
            (z * X_SIZE + (x + offset) % X_SIZE, z * X_SIZE + x)
            for z in range(z_size)
            for x in range(X_SIZE)
        ]
        return lax.ppermute(array, "prefix", pairs)

    right = from_offset(kv, 1)
    left = from_offset(kv_out, -1)
    opposite = from_offset(right, 1)
    recv = lax.all_to_all(
        send, "prefix", split_axis=0, concat_axis=0, axis_index_groups=z_groups, tiled=True
    )
    suffix_rows = suffix_cache[:, 0].transpose(0, 2, 1)
    suffix_out, suffix_lse = suffix_attention(suffix_lengths, q3, suffix_rows)
    recv, suffix_out, suffix_lse = lax.optimization_barrier((recv, suffix_out, suffix_lse))
    ret = prefix_attention(recv, (kv, right, left))
    ret = prefix_attention(recv, (opposite,), ret)
    homed = lax.all_to_all(
        ret, "prefix", split_axis=0, concat_axis=0, axis_index_groups=z_groups, tiled=True
    )
    core = (lax.axis_index("tensor").astype(jnp.int32) % CORES).reshape(1)
    parts = merge_project(core, codes, homed, suffix_out, suffix_lse, out_proj.T, tensor_size)
    y_groups = [[y * CORES + c for y in range(tensor_size // CORES)] for c in range(CORES)]
    parts = lax.all_to_all(
        parts, "tensor", split_axis=0, concat_axis=0, axis_index_groups=y_groups, tiled=True
    )
    parts = jnp.sum(parts.astype(jnp.float32), axis=0).astype(jnp.bfloat16)
    return parts.reshape(STEPS, queries.shape[0], -1).transpose(1, 0, 2)


def solution(mesh):
    return jax.shard_map(
        shards,
        mesh=mesh,
        in_specs=(
            P("prefix", None, "tensor"),
            P("prefix", "tensor", None, None),
            P("prefix", "tensor", None, None),
            P("prefix"),
            P(),
            P(),
            P("tensor", None),
        ),
        out_specs=P("prefix", None, "tensor"),
        check_vma=False,
    )
```

```python
import functools

import jax
import jax.numpy as jnp
from jax import lax
from jax.experimental import pallas as pl
from jax.experimental.pallas import tpu as pltpu
from jax.sharding import PartitionSpec as P

LANES = 128
HALF = 64
X_SIZE = 4
CORES = 2
CAPACITY = 2
GROUPS = X_SIZE * CAPACITY
STEPS = 3
ROWS = 12
PAD_ROWS = 16
SCALE = 0.125
VMEM_LIMIT = 56 * 1024 * 1024
SMALL_LIMIT = 32 * 1024 * 1024
MERGE_LIMIT = 52 * 1024 * 1024


def lane_iota(rows):
    return lax.broadcasted_iota(jnp.int32, (rows, LANES), 1)


def split_heads(rows):
    low = lane_iota(rows.shape[0]) < HALF
    even = jnp.where(low, rows, 0.0)
    odd = jnp.where(low, pltpu.roll(rows, HALF, 1), 0.0)
    return even, odd


def join_heads(even, odd):
    low = lane_iota(even.shape[0]) < HALF
    return jnp.where(low, pltpu.roll(even, HALF, 1), odd)


def nt_dot(left, right):
    return lax.dot_general(
        left, right, (((1,), (1,)), ((), ())), preferred_element_type=jnp.float32
    )


def spread_queries(q_ref, qs):
    requests = q_ref.shape[1]
    for i in range(PAD_ROWS):
        if i < ROWS:
            step, pair = divmod(i, ROWS // STEPS)
            value = q_ref[step, :, pair * LANES : (pair + 1) * LANES].astype(jnp.float32)
        else:
            value = jnp.zeros((requests, LANES), jnp.float32)
        qs[pl.ds(i, requests, stride=PAD_ROWS), :] = value


def route_kernel(me_ref, prefix_ref, owner_ref, q_ref, send_ref, code_ref, taken, source, qs, acc):
    requests = q_ref.shape[1]
    z_size = send_ref.shape[0]
    me = me_ref[0]
    x_own = me & (X_SIZE - 1)
    for i in range(owner_ref.shape[0]):
        taken[i] = 0
    for i in range(z_size * GROUPS):
        source[i] = 0

    def place(r, _):
        name = prefix_ref[me * requests + r]
        owner = owner_ref[name]
        rank = taken[name]
        taken[name] = rank + 1
        offset = (owner - x_own) & (X_SIZE - 1)
        code = (owner >> 2) * GROUPS + (offset ^ (offset >> 1)) * CAPACITY + rank
        code_ref[r] = code
        source[code] = r
        return 0

    lax.fori_loop(0, requests, place, 0, unroll=8)
    spread_queries(q_ref, qs)

    def fill(z, _):
        for slot in range(GROUPS):
            r = source[z * GROUPS + slot]
            block = qs[pl.ds(pl.multiple_of(r * PAD_ROWS, PAD_ROWS), PAD_ROWS), :]
            acc[z, slot * ROWS : (slot + 1) * ROWS, :] = block[:ROWS]
        return 0

    lax.fori_loop(0, z_size, fill, 0, unroll=4)
    send_ref[...] = acc[...].astype(jnp.bfloat16)


def route(me, prefixes, owner, q3, z_size):
    requests = q3.shape[1]
    smem = pl.BlockSpec(memory_space=pltpu.SMEM)
    vmem = pl.BlockSpec(memory_space=pltpu.VMEM)
    shape = (z_size, GROUPS * ROWS, LANES)
    return pl.pallas_call(
        route_kernel,
        out_shape=(
            jax.ShapeDtypeStruct(shape, jnp.bfloat16),
            jax.ShapeDtypeStruct((requests,), jnp.int32),
        ),
        in_specs=[smem, smem, smem, vmem],
        out_specs=(vmem, smem),
        scratch_shapes=[
            pltpu.SMEM((owner.shape[0],), jnp.int32),
            pltpu.SMEM((z_size * GROUPS,), jnp.int32),
            pltpu.VMEM((requests * PAD_ROWS, LANES), jnp.float32),
            pltpu.VMEM(shape, jnp.float32),
        ],
        compiler_params=pltpu.CompilerParams(vmem_limit_bytes=VMEM_LIMIT),
        name="route",
    )(me, prefixes, owner, q3)


SUFFIX_BLOCK = 4


def suffix_kernel(length_ref, q_ref, kv_ref, out_ref, lse_ref, qs):
    spread_queries(q_ref, qs)
    requests, positions, _ = kv_ref.shape
    rows = SUFFIX_BLOCK * PAD_ROWS
    shape = (2 * rows, SUFFIX_BLOCK * positions)
    row = lax.broadcasted_iota(jnp.int32, shape, 0) % rows
    request = row // PAD_ROWS
    step = row % PAD_ROWS // (ROWS // STEPS)
    place = lax.broadcasted_iota(jnp.int32, shape, 1) - request * positions
    past = jnp.where(place >= 0, place - step, 2 * positions)
    request_rows = lax.broadcasted_iota(jnp.int32, (2 * rows, 1), 0) % rows // PAD_ROWS
    low = lane_iota(rows) < HALF

    def some(i, _):
        here = pl.ds(pl.multiple_of(i * rows, rows), rows)
        even, odd = split_heads(qs[here, :] * SCALE)
        query = jnp.concatenate([even, odd], axis=0).astype(jnp.bfloat16)
        cache = kv_ref[pl.ds(i * SUFFIX_BLOCK, SUFFIX_BLOCK)].reshape(-1, LANES)
        limit = jnp.zeros((2 * rows, 1), jnp.int32)
        for r in range(SUFFIX_BLOCK):
            limit = jnp.where(request_rows == r, length_ref[i * SUFFIX_BLOCK + r] - (STEPS - 1), limit)
        scores = jnp.where(past < limit, nt_dot(query, cache), -jnp.inf)
        highest = jnp.max(scores, axis=1, keepdims=True)
        weight = jnp.exp(scores - highest)
        total = jnp.sum(weight, axis=1, keepdims=True)
        mixed = jnp.dot(weight.astype(jnp.bfloat16), cache, preferred_element_type=jnp.float32)
        mixed = mixed / total
        lse = highest + jnp.log(total)
        out_ref[here, :] = join_heads(mixed[:rows], mixed[rows:])
        lse_ref[here, :] = jnp.where(low, lse[:rows], lse[rows:])
        return 0

    lax.fori_loop(0, requests // SUFFIX_BLOCK, some, 0, unroll=2)


def suffix_attention(lengths, q3, kv):
    requests = kv.shape[0]
    vmem = pl.BlockSpec(memory_space=pltpu.VMEM)
    shape = jax.ShapeDtypeStruct((requests * PAD_ROWS, LANES), jnp.float32)
    return pl.pallas_call(
        suffix_kernel,
        out_shape=(shape, shape),
        in_specs=[pl.BlockSpec(memory_space=pltpu.SMEM), vmem, vmem],
        out_specs=(vmem, vmem),
        scratch_shapes=[pltpu.VMEM((requests * PAD_ROWS, LANES), jnp.float32)],
        compiler_params=pltpu.CompilerParams(vmem_limit_bytes=VMEM_LIMIT),
        cost_estimate=pl.CostEstimate(
            flops=8_000_000_000, bytes_accessed=8_000_000, transcendentals=0
        ),
        name="suffix",
    )(lengths, q3, kv)


CHUNKS = 2


def prefix_kernel(count, start, recv_ref, *refs):
    sources = refs[: len(refs) - 8]
    ret_ref, cache, values, queries, acc, stage_out, sems, out_sem = refs[-8:]
    index = pl.program_id(0)
    z_size = recv_ref.shape[0]
    span = CAPACITY * ROWS
    rows = z_size * span
    if start:
        places = [cache.at[0, :HALF], cache.at[0, HALF:]]
    else:
        places = [cache.at[i] for i in range(count)]
    copies = [
        pltpu.make_async_copy(source, place, sems.at[i])
        for i, (source, place) in enumerate(zip(sources, places))
    ]

    @pl.when(index == 0)
    def _():
        for copy in copies:
            copy.start()
        queries[...] = recv_ref[...].astype(jnp.float32) * SCALE
        values[HALF:, :] = jnp.ones_like(values[HALF:, :])
        acc[...] = jnp.zeros_like(acc)

    group = index + (X_SIZE - count if start else 0)
    for i in range(count):

        @pl.when(index == i)
        def _():
            for copy in copies if start else copies[i : i + 1]:
                copy.wait()

    values[:HALF, :] = cache[index, HALF:]
    place = pl.ds(pl.multiple_of(group * span, 8), span)
    own_place = pl.ds(pl.multiple_of(index * span, 8), span)
    query = jnp.concatenate(split_heads(queries[:, place, :].reshape(rows, LANES)), axis=0)
    query = query.astype(jnp.bfloat16)
    size = 2 * rows // CHUNKS
    scores, weights, mixes = [None] * CHUNKS, [None] * CHUNKS, []
    for stage in range(CHUNKS + 2):
        if stage < CHUNKS:
            here = query[stage * size : (stage + 1) * size]
            scores[stage] = jnp.dot(here, cache[index], preferred_element_type=jnp.float32)
        if stage >= 2:
            weight, highest = weights[stage - 2]
            mixed = nt_dot(weight, values[...])
            low = lane_iota(size) < HALF
            total = jnp.where(low, pltpu.roll(mixed, HALF, 1), mixed)
            mixes.append((mixed / total, highest + jnp.log(total)))
        if 1 <= stage <= CHUNKS:
            highest = jnp.max(scores[stage - 1], axis=1, keepdims=True)
            weight = jnp.exp(scores[stage - 1] - highest).astype(jnp.bfloat16)
            weights[stage - 1] = (weight, highest)
    half = CHUNKS // 2
    low = lane_iota(size) < HALF
    lse = []
    for i in range(half):
        out = jnp.where(low, mixes[i][0], pltpu.roll(mixes[i + half][0], HALF, 1))
        sources = slice(i * z_size // half, (i + 1) * z_size // half)
        acc[sources, own_place, :] = out.reshape(z_size // half, span, LANES)
        lse.append(jnp.where(low, mixes[i][1], mixes[i + half][1]))
    lse = jnp.concatenate(lse, axis=0)
    lane = lax.broadcasted_iota(jnp.int32, (span, LANES), 1) & (HALF - 1)
    row = lax.broadcasted_iota(jnp.int32, (span, LANES), 0)
    row = jnp.where(row < ROWS, row, row - ROWS)
    high_part = lse.astype(jnp.bfloat16).astype(jnp.float32)
    rest = lse - high_part
    mid_part = rest.astype(jnp.bfloat16).astype(jnp.float32)
    packed = jnp.zeros((z_size, span, LANES), jnp.float32)
    for i, part in enumerate((high_part, mid_part, rest - mid_part)):
        part = part.reshape(z_size, span, LANES)
        packed = jnp.where((lane == row + i * ROWS)[None], part, packed)
    packed = packed.reshape(rows, LANES).astype(jnp.bfloat16)
    shape = (z_size * GROUPS, rows)
    slot = lax.broadcasted_iota(jnp.int32, shape, 0)
    inside = (slot & (GROUPS - 1)) // CAPACITY == index
    slot = slot // GROUPS * CAPACITY + (slot & (CAPACITY - 1))
    first = lax.broadcasted_iota(jnp.int32, shape, 1) - slot * ROWS
    pick = jnp.logical_and(inside, jnp.logical_and(first >= 0, first < ROWS))
    lse_rows = jnp.dot(pick.astype(jnp.bfloat16), packed, preferred_element_type=jnp.float32)
    lse_rows = lse_rows.reshape(z_size, GROUPS, LANES)
    own = lax.broadcasted_iota(jnp.int32, (GROUPS, LANES), 0) // CAPACITY == index
    acc[:, count * span :, :] = jnp.where(own[None], lse_rows, acc[:, count * span :, :])

    @pl.when(index == count - 1)
    def _():
        stage_out[...] = acc[...].astype(jnp.bfloat16)
        copy = pltpu.make_async_copy(
            stage_out, ret_ref.at[:, start : start + stage_out.shape[1], :], out_sem
        )
        copy.start()
        copy.wait()


FIRST_GROUPS = 3
FIRST_ROWS = FIRST_GROUPS * CAPACITY * ROWS + GROUPS
ALL_ROWS = FIRST_ROWS + CAPACITY * ROWS + GROUPS


def prefix_attention(recv, caches, before=None):
    z_size = recv.shape[0]
    count = len(caches) if before is None else 1
    start = 0 if before is None else FIRST_ROWS
    length = caches[0].shape[1]
    rows = count * CAPACITY * ROWS + GROUPS
    vmem = pl.BlockSpec(memory_space=pltpu.VMEM)
    anywhere = pl.BlockSpec(memory_space=pl.ANY)
    kernel = functools.partial(prefix_kernel, count, start)
    operands = [recv, *caches]
    aliases = {}
    if before is not None:
        aliases = {len(operands): 0}
        operands.append(before)
        inner = kernel
        kernel = lambda *refs: inner(*refs[:3], *refs[4:])
    return pl.pallas_call(
        kernel,
        grid=(count,),
        out_shape=jax.ShapeDtypeStruct((z_size, ALL_ROWS, LANES), jnp.bfloat16),
        in_specs=[vmem] + [anywhere] * (len(operands) - 1),
        out_specs=anywhere,
        scratch_shapes=[
            pltpu.VMEM((count, LANES, length), jnp.bfloat16),
            pltpu.VMEM((LANES, length), jnp.bfloat16),
            pltpu.VMEM(recv.shape, jnp.float32),
            pltpu.VMEM((z_size, rows, LANES), jnp.float32),
            pltpu.VMEM((z_size, rows, LANES), jnp.bfloat16),
            pltpu.SemaphoreType.DMA((len(caches),)),
            pltpu.SemaphoreType.DMA,
        ],
        input_output_aliases=aliases,
        compiler_params=pltpu.CompilerParams(vmem_limit_bytes=SMALL_LIMIT),
        cost_estimate=pl.CostEstimate(
            flops=2_500_000_000 * count, bytes_accessed=1_000_000 * count, transcendentals=0
        ),
        name="prefix",
    )(*operands)


def merge_kernel(core_ref, code_ref, ret_ref, suffix_ref, suffix_lse_ref, w_ref, out_ref, left, wide, picked, packed, merged):
    requests = code_ref.shape[0]

    @pl.when(pl.program_id(0) == 0)
    def _():
        wide[...] = ret_ref[...].astype(jnp.float32)
        pair_rows = CAPACITY * ROWS
        for r in range(requests):
            code = code_ref[r]
            z, slot = code // GROUPS, code % GROUPS
            group = slot // CAPACITY
            last = group == FIRST_GROUPS
            start = pl.multiple_of(jnp.where(last, FIRST_ROWS, group * pair_rows), 8)
            lse_row = slot + jnp.where(
                last, ALL_ROWS - GROUPS - FIRST_GROUPS * CAPACITY, FIRST_ROWS - GROUPS
            )
            pair = wide[z, pl.ds(start, pair_rows), :]
            second = jnp.concatenate([pair[ROWS:], pair[: PAD_ROWS - ROWS]], axis=0)
            picked[r] = jnp.where(slot % CAPACITY == 0, pair[:PAD_ROWS], second)
            packed[r : r + 1, :] = wide[z, pl.ds(lse_row, 1), :]
        lane = lane_iota(PAD_ROWS) % HALF
        row = lax.broadcasted_iota(jnp.int32, (PAD_ROWS, LANES), 0)
        own = jnp.logical_or(lane == row, jnp.logical_or(lane == row + ROWS, lane == row + 2 * ROWS))
        own = jnp.logical_and(own, row < ROWS)
        copies = jnp.where(own[None], packed[...][:, None, :], 0.0).astype(jnp.bfloat16)
        same_half = lax.broadcasted_iota(jnp.int32, (LANES, LANES), 0) // HALF
        same_half = same_half == lane_iota(LANES) // HALF
        prefix_lse = jnp.dot(
            copies.reshape(requests * PAD_ROWS, LANES),
            same_half.astype(jnp.bfloat16),
            preferred_element_type=jnp.float32,
        )
        gap = prefix_lse - suffix_lse_ref[...]
        small = jnp.exp(-jnp.abs(gap))
        large_weight = 1.0 / (1.0 + small)
        small_weight = small * large_weight
        prefix_first = gap >= 0.0
        merged[...] = picked[...].reshape(requests * PAD_ROWS, LANES) * jnp.where(
            prefix_first, large_weight, small_weight
        ) + suffix_ref[...] * jnp.where(prefix_first, small_weight, large_weight)
        pairs = ROWS // STEPS
        for step in range(STEPS):
            for pair in range(pairs):
                left[step * requests : (step + 1) * requests, pair * LANES : (pair + 1) * LANES] = merged[
                    pl.ds(step * pairs + pair, requests, stride=PAD_ROWS), :
                ].astype(jnp.bfloat16)

    for part in range(w_ref.shape[0]):
        out_ref[part] = nt_dot(left[...], w_ref[part, 0]).astype(jnp.bfloat16)


def project_kernel(core_ref, left_ref, w_ref, out_ref):
    for part in range(w_ref.shape[0]):
        out_ref[part] = nt_dot(left_ref[...], w_ref[part, core_ref[0]]).astype(jnp.bfloat16)


def merge_project(core, codes, ret, suffix_out, suffix_lse, weights, parts):
    requests = codes.shape[0]
    width = weights.shape[0] // parts
    depth = weights.shape[1]
    rows = STEPS * requests
    weights = weights.reshape(parts // CORES, CORES, width, depth)
    whole = lambda shape: pl.BlockSpec(shape, lambda t, core: (0,) * len(shape))
    out_spec = whole((parts // CORES, rows, width))
    out_shape = jax.ShapeDtypeStruct((parts // CORES, rows, width), jnp.bfloat16)
    other, left = pl.pallas_call(
        merge_kernel,
        out_shape=(out_shape, jax.ShapeDtypeStruct((rows, depth), jnp.bfloat16)),
        grid_spec=pltpu.PrefetchScalarGridSpec(
            num_scalar_prefetch=1,
            grid=(1,),
            in_specs=[
                pl.BlockSpec(memory_space=pltpu.SMEM),
                whole(ret.shape),
                whole(suffix_out.shape),
                whole(suffix_lse.shape),
                pl.BlockSpec((parts // CORES, 1, width, depth), lambda t, core: (0, 1 - core[0], 0, 0)),
            ],
            out_specs=(out_spec, whole((rows, depth))),
            scratch_shapes=[
                pltpu.VMEM(ret.shape, jnp.float32),
                pltpu.VMEM((requests, PAD_ROWS, LANES), jnp.float32),
                pltpu.VMEM((requests, LANES), jnp.float32),
                pltpu.VMEM((requests * PAD_ROWS, LANES), jnp.float32),
            ],
        ),
        compiler_params=pltpu.CompilerParams(vmem_limit_bytes=MERGE_LIMIT),
        name="merge",
    )(core, codes, ret, suffix_out, suffix_lse, weights)
    received = lax.ppermute(other, "tensor", [(i, i ^ 1) for i in range(parts)])
    vmem = pl.BlockSpec(memory_space=pltpu.VMEM)
    own = pl.pallas_call(
        project_kernel,
        out_shape=out_shape,
        in_specs=[pl.BlockSpec(memory_space=pltpu.SMEM), vmem, vmem],
        out_specs=vmem,
        compiler_params=pltpu.CompilerParams(vmem_limit_bytes=SMALL_LIMIT),
        cost_estimate=pl.CostEstimate(
            flops=2_000_000_000, bytes_accessed=2_000_000, transcendentals=0
        ),
        name="project",
    )(core, left, weights)
    return (own.astype(jnp.float32) + received.astype(jnp.float32)).astype(jnp.bfloat16)


def shards(queries, prefix_cache, suffix_cache, suffix_lengths, request_prefix, prefix_owner, out_proj):
    prefix_size = lax.axis_size("prefix")
    tensor_size = lax.axis_size("tensor")
    z_size = prefix_size // X_SIZE
    z_groups = [[z * X_SIZE + x for z in range(z_size)] for x in range(X_SIZE)]
    me = lax.axis_index("prefix").astype(jnp.int32).reshape(1)
    kv = prefix_cache[0, 0]
    q3 = queries.transpose(1, 0, 2)
    send, codes = route(me, request_prefix.reshape(-1), prefix_owner, q3, z_size)
    kv_out, send = lax.optimization_barrier((kv, send))

    def from_offset(array, offset):
        pairs = [
            (z * X_SIZE + (x + offset) % X_SIZE, z * X_SIZE + x)
            for z in range(z_size)
            for x in range(X_SIZE)
        ]
        return lax.ppermute(array, "prefix", pairs)

    right = from_offset(kv, 1)
    left = from_offset(kv_out, -1)
    opposite = (from_offset(right[:HALF], 1), from_offset(left[HALF:], -1))
    recv = lax.all_to_all(
        send, "prefix", split_axis=0, concat_axis=0, axis_index_groups=z_groups, tiled=True
    )
    suffix_rows = suffix_cache[:, 0].transpose(0, 2, 1)
    suffix_out, suffix_lse = suffix_attention(suffix_lengths, q3, suffix_rows)
    recv, suffix_out, suffix_lse = lax.optimization_barrier((recv, suffix_out, suffix_lse))
    ret = prefix_attention(recv, (kv, right, left))
    ret = prefix_attention(recv, opposite, ret)
    homed = lax.all_to_all(
        ret, "prefix", split_axis=0, concat_axis=0, axis_index_groups=z_groups, tiled=True
    )
    core = (lax.axis_index("tensor").astype(jnp.int32) % CORES).reshape(1)
    parts = merge_project(core, codes, homed, suffix_out, suffix_lse, out_proj.T, tensor_size)
    y_groups = [[y * CORES + c for y in range(tensor_size // CORES)] for c in range(CORES)]
    parts = lax.all_to_all(
        parts, "tensor", split_axis=0, concat_axis=0, axis_index_groups=y_groups, tiled=True
    )
    parts = jnp.sum(parts.astype(jnp.float32), axis=0).astype(jnp.bfloat16)
    return parts.reshape(STEPS, queries.shape[0], -1).transpose(1, 0, 2)


def solution(mesh):
    return jax.shard_map(
        shards,
        mesh=mesh,
        in_specs=(
            P("prefix", None, "tensor"),
            P("prefix", "tensor", None, None),
            P("prefix", "tensor", None, None),
            P("prefix"),
            P(),
            P(),
            P("tensor", None),
        ),
        out_specs=P("prefix", None, "tensor"),
        check_vma=False,
    )
```
